512 devices in a mesh: replica: 8 (over z_hi, x), section: 8 (over y, core), tensor: 8 (over z_lo).
Axes of the slice: x: 4, y: 4, z: 16 (z_hi: 2, z_lo: 8; z = z_hi * 8 + z_lo), core: 2. Of those that a mesh axis runs over, the one named last changes fastest.
Arguments:
- activations: bfloat16 [8, 8, 512, 4096], P('replica', 'section', None, 'tensor'), may hold values from -6 to 6
- key_grads: bfloat16 [8, 8, 512, 512], P('replica', 'section', None, 'tensor'), may hold values from -6 to 6
- weight: bfloat16 [8, 8, 512, 4096], P('replica', 'section', 'tensor'), may hold values from -0.09375 to 0.09375
- first_moment: float32 [8, 8, 512, 4096], P('replica', 'section', 'tensor'), may hold values from -10 to 10
- second_moment: float32 [8, 8, 512, 4096], P('replica', 'section', 'tensor'), may hold values from 0.5 to 10
- probe_matrix: float32 [128, 8], replicated, may hold values from -6 to 6
- failed_replica: int32 [8, 8], replicated, may hold values from 0 to 7
- resend_spans: int32 [8, 8], replicated, may hold values from 0 to 31, as said below
Outputs:
- key_out: bfloat16 [8, 8, 512, 512], P('replica', 'section', None, 'tensor')
- input_grads: bfloat16 [8, 8, 512, 4096], P('replica', 'section', None, 'tensor')
- update: float32 [8, 8, 512, 4096], P('replica', 'section', 'tensor')
- checksums: float32 [8, 8, 2, 512, 256], P('replica', 'section', None, 'tensor')
- weight_checksums: float32 [8, 8, 512, 256], P('replica', 'section', 'tensor')
The draws below stay inside these ranges and needn't reach their ends.
Inputs may be any that keep to these rules, and one draw needn't show every extreme that they name: `resend_spans`: each row holds 8 distinct span numbers.
All inputs are finite; a program needn't handle non-finite values.
Results may differ from the reference program's by a relative error of at most 0.014.
Values may be sent and summed in bfloat16 or wider, within the bound.
No kernel may reach another device: no remote copies, remote signals or barrier semaphores. Data moves between devices by JAX's collectives and lax.ppermute only.
A program may use at most 64 MiB of HBM per device.

```python
import math
import jax
import jax.numpy as jnp
from jax import lax

D = 4096
KD = 512
TOK_DEV = 512
RESENDS = 8
PROBES = 8
COPIES = 8
SECTIONS = 8
TPAR = 8
N_TENSOR = 8


def draw_resend_spans(key, part):
    key = jax.random.fold_in(key, 7)
    section_keys = jax.random.split(key, SECTIONS)

    def one_section(section_key):
        order = jax.random.permutation(section_key, D // 128)
        return order[:RESENDS]
    return jax.vmap(one_section)(section_keys).astype(jnp.int32)


def place_ends(array, stream_key, smallest, high):
    spot = [jax.random.randint(jax.random.fold_in(stream_key, axis), (), 0, length) for axis, length in enumerate(array.shape)]
    widest = array.shape.index(max(array.shape))
    neighbour = spot[:widest] + [(spot[widest] + 1) % array.shape[widest]] + spot[widest + 1:]
    return array.at[tuple(spot)].set(smallest).at[tuple(neighbour)].set(high)


def block_scale(rng, extent, shards, low, high):
    factor_of, own = 1.0, jax.random.fold_in(rng, 6)
    for position, shards_of in shards:
        heights = jnp.exp(jax.random.uniform(jax.random.fold_in(own, position), (shards_of,), jnp.float32, low / len(shards), high / len(shards)))
        factor_of = factor_of * jnp.repeat(heights, extent[position] // shards_of).reshape([-1 if axis == position else 1 for axis in range(len(extent))])
    return factor_of


def normal_values(key, extent, deviation, reach, pieces=(), held_as=jnp.bfloat16):
    values = jax.random.normal(key, extent, jnp.float32) * deviation
    if len(pieces) > 0:
        values = block_scale(key, extent, pieces, -0.22, 0.18) * values
    return jnp.clip(values, min=-reach, max=reach).astype(held_as)


def setup_inputs(seed: int = 0) -> dict:
    key_list = jax.random.split(jax.random.key(seed), 9)
    activations = normal_values(key_list[0], (COPIES, SECTIONS, TOK_DEV, D), 1.0, 6.0, ((0, 8), (1, 8), (3, 8)))
    key_grads = normal_values(key_list[1], (COPIES, SECTIONS, TOK_DEV, KD), 1.0, 6.0, ((0, 8), (1, 8), (3, 8)))
    weight = normal_values(key_list[2], (COPIES, SECTIONS, KD, D), D ** -0.5, 0.09375, ((0, 8), (1, 8), (2, 8)))
    first_moment = normal_values(key_list[3], (COPIES, SECTIONS, KD, D), 2.0, 10.0, ((0, 8), (1, 8), (2, 8)), jnp.float32)
    second_moment = jnp.clip(jnp.exp(math.log(10.0) - 2.9957323 * jax.random.uniform(key_list[4], (COPIES, SECTIONS, KD, D), jnp.float32) ** block_scale(key_list[4], (COPIES, SECTIONS, KD, D), ((0, 8), (1, 8), (2, 8)), -0.2, 0.2)), 0.5, 10.0)
    probe_matrix = normal_values(key_list[5], (128, PROBES), 1.0, 6.0, (), jnp.float32)
    failed_replica = place_ends(jax.random.randint(key_list[6], (SECTIONS, TPAR), 0, COPIES), jax.random.fold_in(key_list[6], 1), 0, COPIES - 1).astype(jnp.int32)
    resend_spans = draw_resend_spans(jax.random.fold_in(key_list[8], 71), 0)
    return {"activations": activations, "key_grads": key_grads, "weight": weight, "first_moment": first_moment, "second_moment": second_moment, "probe_matrix": probe_matrix, "failed_replica": failed_replica, "resend_spans": resend_spans}


def checksum_of(source, probe_matrix):
    nchunk = D // 128
    shaped = source.reshape(COPIES, SECTIONS, KD, nchunk, 128)
    mixed = jnp.einsum('rsjnc,cp->rsjnp', shaped, probe_matrix, precision=lax.Precision.HIGHEST)
    return mixed.reshape(COPIES, SECTIONS, KD, nchunk * PROBES)

def reference(activations, key_grads, weight, first_moment, second_moment, probe_matrix, failed_replica, resend_spans):
    per_device = KD // N_TENSOR
    nchunk = D // 128
    row_group = jnp.arange(KD, dtype=jnp.int32) // per_device
    failed_rows = failed_replica[:, row_group]
    primary = jnp.bitwise_xor(failed_rows, COPIES // 2)
    second = jnp.bitwise_xor(failed_rows, 1)
    listed = jnp.any(resend_spans[:, :, None] == jnp.arange(nchunk, dtype=jnp.int32)[None, None, :], axis=1)
    columns = jnp.repeat(listed, 128, axis=1)
    replica_ids = jnp.arange(COPIES, dtype=jnp.int32)

    def restore(source):
        from_primary = jnp.zeros(source.shape[1:], source.dtype)
        from_second = jnp.zeros(source.shape[1:], source.dtype)
        for index in range(COPIES):
            from_primary = jnp.where((primary == index)[:, :, None], source[index], from_primary)
            from_second = jnp.where((second == index)[:, :, None], source[index], from_second)
        fresh = jnp.where(columns[:, None, :], from_second, from_primary)
        hit = replica_ids[:, None, None, None] == failed_rows[None, :, :, None]
        return jnp.where(hit, fresh[None], source)
    restored_weight = restore(weight)
    restored_first = restore(first_moment)
    restored_second = restore(second_moment)
    incoming = jnp.roll(activations, 1, axis=1).astype(jnp.float32)
    inverse_rms = 1.0 / jnp.sqrt(lax.optimization_barrier(jnp.mean(incoming * incoming, axis=-1, keepdims=True)) + 1e-05)
    normed = (incoming * inverse_rms).astype(jnp.bfloat16)
    key_out = jnp.einsum('rstd,rskd->rstk', normed.astype(jnp.float32), restored_weight.astype(jnp.float32)).astype(jnp.bfloat16)
    local_grads = jnp.einsum('rstk,rstd->rskd', key_grads.astype(jnp.float32), normed.astype(jnp.float32))
    mean_grad = lax.optimization_barrier(jnp.sum(local_grads, axis=0)) / COPIES
    moment_one = 0.9 * restored_first + 0.1 * mean_grad[None]
    moment_two = 0.95 * restored_second + 0.05 * (mean_grad * mean_grad)[None]
    update = moment_one / (jnp.sqrt(moment_two) + 1e-08)
    feature_grads = jnp.zeros((COPIES, SECTIONS, TOK_DEV, D), jnp.float32)
    for shard_index in range(N_TENSOR):
        lower = shard_index * per_device
        partial_value = jnp.einsum('rstk,rskd->rstd', key_grads[..., lower:lower + per_device].astype(jnp.float32), restored_weight[:, :, lower:lower + per_device].astype(jnp.float32))
        feature_grads = feature_grads + lax.optimization_barrier(partial_value.astype(jnp.bfloat16)).astype(jnp.float32)
    product = lax.optimization_barrier(jnp.sum(feature_grads * incoming, axis=-1, keepdims=True))
    back = inverse_rms * feature_grads - inverse_rms * inverse_rms * inverse_rms * incoming * product / D
    input_grads = jnp.roll(back.astype(jnp.bfloat16), -1, axis=1)
    checksums = jnp.stack([checksum_of(restored_first, probe_matrix), checksum_of(restored_second, probe_matrix)], axis=2)
    weight_checksums = checksum_of(restored_weight.astype(jnp.float32), probe_matrix)
    return (key_out, input_grads, update, checksums, weight_checksums)
```

```python
import jax
import jax.numpy as jnp
from jax import lax
from jax.sharding import PartitionSpec as P

SHORT = jnp.bfloat16
WIDE = jnp.float32
PLANE = 4


def from_behind(block, axis, distance):
    n = lax.axis_size(axis)
    return lax.ppermute(block, axis, [((i - distance) % n, i) for i in range(n)])


def swap(block, axis, bit):
    return lax.ppermute(block, axis, [(i, i ^ bit) for i in range(lax.axis_size(axis))])


def exchange_x(block):
    groups = [[0, 1, 2, 3], [4, 5, 6, 7]]
    return lax.all_to_all(block, "replica", 0, 0, axis_index_groups=groups, tiled=True)


def two_halves(value):
    high = value.astype(SHORT)
    return high, (value - high.astype(WIDE)).astype(SHORT)


def gather_tensor(block):
    held = block[None]
    for bit in (4, 2, 1):
        held = jnp.concatenate([held, swap(held, "tensor", bit)], axis=0)
    order = (0, 4, 2, 6, 1, 5, 3, 7)
    held = jnp.stack([held[order.index(i)] for i in range(8)])
    mine = lax.axis_index("tensor")
    for bit in (4, 2, 1):
        shape = (8 // (2 * bit), 2, bit) + block.shape
        split = held.reshape(shape)
        held = jnp.where((mine & bit) != 0, split[:, ::-1], split).reshape(held.shape)
    return held


def adam(first, second, grad):
    one = 0.9 * first + 0.1 * grad
    two = 0.95 * second + 0.05 * (grad * grad)
    return one / (jnp.sqrt(two) + 1e-08)


def shards(activations, key_grads, weight, first_moment, second_moment, probe_matrix, failed_replica, resend_spans):
    copies = lax.axis_size("replica")
    my_replica = lax.axis_index("replica")
    my_section = lax.axis_index("section")
    my_tensor = lax.axis_index("tensor")
    failed = failed_replica[my_section, my_tensor]
    my_spans = resend_spans[my_section]
    own_weight = weight[0, 0]
    own_first = first_moment[0, 0]
    own_second = second_moment[0, 0]
    rows, width = own_weight.shape
    nchunk = width // 128
    listed = jnp.any(my_spans[:, None] == jnp.arange(nchunk, dtype=jnp.int32)[None, :], axis=0)
    columns = jnp.repeat(listed, 128)[None, :]
    primary = jnp.bitwise_xor(failed, PLANE)
    second = jnp.bitwise_xor(failed, 1)
    chosen = jnp.where(columns, my_replica == second, my_replica == primary)
    is_failed = my_replica == failed
    part = rows // PLANE

    local = activations[0, 0]
    tokens, cols = local.shape
    incoming = from_behind(local, "section", 1)
    squares = jnp.sum(jnp.square(local.astype(WIDE)), axis=1)
    high, low = two_halves(squares)
    extra = jnp.concatenate([high[None], low[None], jnp.zeros((6, tokens), SHORT)], axis=0)
    kg_rows = jnp.concatenate([key_grads[0, 0].T, extra], axis=0)
    kg_rows = gather_tensor(kg_rows)
    kg_all = kg_rows[:, :rows].reshape(8 * rows, tokens)
    total = jnp.sum(kg_rows[:, rows].astype(WIDE) + kg_rows[:, rows + 1].astype(WIDE), axis=0)
    total = from_behind(total.reshape(-1, 128), "section", 1).reshape(tokens)
    inverse_rms = 1.0 / jnp.sqrt(total / width + 1e-05)

    masked = [jnp.where(chosen, a.astype(SHORT), 0).reshape(PLANE, 1, part, width) for a in (own_weight, own_first, own_second)]
    spread = exchange_x(jnp.concatenate(masked, axis=1))
    spread = jnp.sum(spread.astype(WIDE), axis=0).astype(SHORT)
    fresh_weight = spread[0] + swap(spread[0], "replica", PLANE)
    fresh_moments = spread[1:] + swap(spread[1:], "replica", PLANE)
    groups = [[0, 1, 2, 3], [4, 5, 6, 7]]
    fresh_weight = lax.all_gather(fresh_weight, "replica", axis=0, tiled=True, axis_index_groups=groups)
    restored_weight = jnp.where(is_failed, fresh_weight, own_weight)

    x = incoming.astype(WIDE)
    normed = (x * inverse_rms[:, None]).astype(SHORT)
    grad = lax.dot_general(kg_all, normed, (((1,), (0,)), ((), ())), preferred_element_type=WIDE).astype(SHORT)
    grad = grad.reshape(8, PLANE, part, cols).transpose(1, 0, 2, 3)
    grad = jnp.sum(exchange_x(grad).astype(WIDE), axis=0).astype(SHORT)

    sent = jnp.concatenate([restored_weight.reshape(rows, 8, cols).transpose(1, 0, 2), grad], axis=1)
    got = lax.all_to_all(sent, "tensor", 0, 0, tiled=True)
    weight_cols = got[:, :rows].reshape(8 * rows, cols)
    grad_rows = got[:, rows:].transpose(1, 0, 2).reshape(part, width)
    mean_rows = (grad_rows.astype(WIDE) + swap(grad_rows, "replica", PLANE).astype(WIDE)) / copies

    keys = lax.dot_general(weight_cols, normed, (((1,), (1,)), ((), ())), preferred_element_type=WIDE).astype(SHORT)
    feature = lax.dot_general(kg_all, weight_cols, (((0,), (0,)), ((), ())), preferred_element_type=WIDE)
    high, low = two_halves(jnp.sum(feature * x, axis=1))
    extra = jnp.concatenate([high[None], low[None], jnp.zeros((6, tokens), SHORT)], axis=0)
    sent = jnp.concatenate([keys.reshape(8, rows, tokens), jnp.broadcast_to(extra[None], (8, 8, tokens))], axis=1)
    got = jnp.sum(lax.all_to_all(sent, "tensor", 0, 0, tiled=True).astype(WIDE), axis=0)
    key_out = got[:rows].T.astype(SHORT)
    product = (got[rows] + got[rows + 1])[:, None]
    scale = inverse_rms[:, None]
    input_grad = scale * feature - scale * scale * scale * x * product / width
    outgoing = from_behind(input_grad.astype(SHORT), "section", -1)

    def checksum(source):
        shaped = source.reshape(-1, nchunk, 128)
        mixed = jnp.einsum("jnc,cp->jnp", shaped, probe_matrix, precision=lax.Precision.HIGHEST)
        return mixed.reshape(-1, nchunk * probe_matrix.shape[1])

    fresh = fresh_moments.astype(WIDE)
    fresh_update = adam(fresh[0], fresh[1], mean_rows).astype(SHORT)
    fresh_sums = checksum(fresh.reshape(2 * part, width)).astype(SHORT).reshape(2, width)
    shared = jnp.concatenate([mean_rows.astype(SHORT), fresh_update, fresh_sums], axis=0)
    shared = exchange_x(jnp.broadcast_to(shared[None], (PLANE,) + shared.shape))
    mean_grad = shared[:, :part].reshape(rows, width).astype(WIDE)
    fresh_update = shared[:, part : 2 * part].reshape(rows, width).astype(WIDE)
    fresh_sums = shared[:, 2 * part :].reshape(PLANE, 2, part, -1).transpose(1, 0, 2, 3).reshape(2, rows, -1).astype(WIDE)
    update = jnp.where(is_failed, fresh_update, adam(own_first, own_second, mean_grad))
    own_sums = jnp.stack([checksum(own_first), checksum(own_second)])
    checksums = jnp.where(is_failed, fresh_sums, own_sums)
    weight_checksums = checksum(restored_weight.astype(WIDE))
    return (key_out[None, None], outgoing[None, None], update[None, None], checksums[None, None], weight_checksums[None, None])


def solution(mesh):
    by_rows = P("replica", "section", "tensor", None)
    by_features = P("replica", "section", None, "tensor")
    return jax.shard_map(
        shards,
        mesh=mesh,
        in_specs=(by_features, by_features, by_rows, by_rows, by_rows, P(), P(), P()),
        out_specs=(by_features, by_features, by_rows, P("replica", "section", None, "tensor", None), by_rows),
        check_vma=False,
    )
```

```python
import jax
import jax.numpy as jnp
from jax import lax
from jax.sharding import PartitionSpec as P

SHORT = jnp.bfloat16
WIDE = jnp.float32
PLANE = 4


def from_behind(block, axis, distance):
    n = lax.axis_size(axis)
    return lax.ppermute(block, axis, [((i - distance) % n, i) for i in range(n)])


def swap(block, axis, bit):
    return lax.ppermute(block, axis, [(i, i ^ bit) for i in range(lax.axis_size(axis))])


def exchange_x(block):
    groups = [[0, 1, 2, 3], [4, 5, 6, 7]]
    return lax.all_to_all(block, "replica", 0, 0, axis_index_groups=groups, tiled=True)


def two_halves(value):
    high = value.astype(SHORT)
    return high, (value - high.astype(WIDE)).astype(SHORT)


def in_order(held, mine, bits):
    for bit in bits:
        split = held.reshape((held.shape[0] // (2 * bit), 2, bit) + held.shape[1:])
        held = jnp.where((mine & bit) != 0, split[:, ::-1], split).reshape(held.shape)
    return held


def doubled(held, mine, axis):
    bit = 4 >> axis
    came = swap(held, "tensor", bit)
    high = (mine & bit) != 0
    return jnp.stack([jnp.where(high, came, held), jnp.where(high, held, came)], axis=axis)


def gather_x(block):
    held = jnp.stack([block] + [swap(block, "replica", bit) for bit in (1, 2, 3)])
    return in_order(held, lax.axis_index("replica") & 3, (2, 1))


def broadcast_x(block):
    return exchange_x(jnp.broadcast_to(block[None], (PLANE,) + block.shape))


def tied(value, *after):
    return lax.optimization_barrier((value,) + after)[0]


def adam(first, second, grad):
    one = 0.9 * first + 0.1 * grad
    two = 0.95 * second + 0.05 * (grad * grad)
    return one / (jnp.sqrt(two) + 1e-08)


def shards(activations, key_grads, weight, first_moment, second_moment, probe_matrix, failed_replica, resend_spans):
    copies = lax.axis_size("replica")
    my_replica = lax.axis_index("replica")
    my_section = lax.axis_index("section")
    my_tensor = lax.axis_index("tensor")
    failed = failed_replica[my_section, my_tensor]
    my_spans = resend_spans[my_section]
    own_weight = weight[0, 0]
    own_first = first_moment[0, 0]
    own_second = second_moment[0, 0]
    rows, width = own_weight.shape
    nchunk = width // 128
    listed = jnp.any(my_spans[:, None] == jnp.arange(nchunk, dtype=jnp.int32)[None, :], axis=0)
    columns = jnp.repeat(listed, 128)[None, :]
    primary = jnp.bitwise_xor(failed, PLANE)
    second = jnp.bitwise_xor(failed, 1)
    chosen = jnp.where(columns, my_replica == second, my_replica == primary)
    is_failed = my_replica == failed
    part = rows // PLANE

    def masked(block):
        return jnp.where(chosen, block.astype(SHORT), 0).reshape(PLANE, 1, part, width)

    def summed(parts):
        return jnp.sum(parts.astype(WIDE), axis=0).astype(SHORT)

    mask_weight = masked(own_weight)
    spread_weight = summed(exchange_x(mask_weight))[0]
    mask_moments = jnp.concatenate([masked(own_first), masked(own_second)], axis=1)

    local = activations[0, 0]
    tokens, cols = local.shape
    squares = jnp.sum(jnp.square(local.astype(WIDE)), axis=1)
    high, low = two_halves(squares)
    extra = jnp.concatenate([high[None], low[None], jnp.zeros((6, tokens), SHORT)], axis=0)
    held = jnp.concatenate([key_grads[0, 0].T, extra], axis=0)
    held = tied(held, mask_weight)
    incoming = from_behind(tied(local, held), "section", 1)
    held = doubled(doubled(held, my_tensor, 0), my_tensor, 1)
    held, spread_weight = lax.optimization_barrier((held, spread_weight))
    fresh_weight = spread_weight + swap(spread_weight, "replica", PLANE)
    spread_moments = summed(exchange_x(tied(mask_moments, spread_weight)))
    held = doubled(held, my_tensor, 2)
    held, fresh_weight = lax.optimization_barrier((held, fresh_weight))
    kg_rows = held.reshape((8,) + held.shape[3:])
    kg_all = kg_rows[:, :rows].reshape(8 * rows, tokens)
    total = jnp.sum(kg_rows[:, rows].astype(WIDE) + kg_rows[:, rows + 1].astype(WIDE), axis=0)
    total = from_behind(total.reshape(-1, 128), "section", 1).reshape(tokens)
    inverse_rms = 1.0 / jnp.sqrt(total / width + 1e-05)

    spread_moments = tied(spread_moments, fresh_weight)
    fresh_moments = spread_moments + swap(spread_moments, "replica", PLANE)
    fresh_weight = broadcast_x(tied(fresh_weight, spread_moments)).reshape(rows, width)
    restored_weight = jnp.where(is_failed, fresh_weight, own_weight)

    x = incoming.astype(WIDE)
    normed = (x * inverse_rms[:, None]).astype(SHORT)
    grad = lax.dot_general(kg_all, normed, (((1,), (0,)), ((), ())), preferred_element_type=WIDE).astype(SHORT)
    grad = tied(grad, restored_weight, fresh_moments)
    grad = grad.reshape(8, PLANE, part, cols).transpose(1, 0, 2, 3)
    grad = jnp.sum(exchange_x(grad).astype(WIDE), axis=0).astype(SHORT)

    sent = jnp.concatenate([restored_weight.reshape(rows, 8, cols).transpose(1, 0, 2), grad], axis=1)
    got = lax.all_to_all(sent, "tensor", 0, 0, tiled=True)
    weight_cols = got[:, :rows].reshape(8 * rows, cols)
    grad_rows = got[:, rows:].transpose(1, 0, 2).reshape(part, width)
    mean_rows = (grad_rows.astype(WIDE) + swap(grad_rows, "replica", PLANE).astype(WIDE)) / copies

    keys = lax.dot_general(weight_cols, normed, (((1,), (1,)), ((), ())), preferred_element_type=WIDE).astype(SHORT)
    feature = lax.dot_general(kg_all, weight_cols, (((0,), (0,)), ((), ())), preferred_element_type=WIDE)
    high, low = two_halves(jnp.sum(feature * x, axis=1))
    extra = jnp.concatenate([high[None], low[None], jnp.zeros((6, tokens), SHORT)], axis=0)
    sent = jnp.concatenate([keys.reshape(8, rows, tokens), jnp.broadcast_to(extra[None], (8, 8, tokens))], axis=1)
    got = jnp.sum(lax.all_to_all(sent, "tensor", 0, 0, tiled=True).astype(WIDE), axis=0)
    key_out = got[:rows].T.astype(SHORT)
    product = (got[rows] + got[rows + 1])[:, None]
    scale = inverse_rms[:, None]
    input_grad = scale * feature - scale * scale * scale * x * product / width
    outgoing = from_behind(input_grad.astype(SHORT), "section", -1)

    def checksum(source):
        shaped = source.reshape(-1, nchunk, 128)
        mixed = jnp.einsum("jnc,cp->jnp", shaped, probe_matrix, precision=lax.Precision.HIGHEST)
        return mixed.reshape(-1, nchunk * probe_matrix.shape[1])

    fresh = fresh_moments.astype(WIDE)
    fresh_update = adam(fresh[0], fresh[1], mean_rows).astype(SHORT)
    fresh_sums = checksum(fresh.reshape(2 * part, width)).astype(SHORT).reshape(2, width)
    shared = jnp.concatenate([mean_rows.astype(SHORT), fresh_update, fresh_sums], axis=0)
    shared = gather_x(shared)
    mean_grad = shared[:, :part].reshape(rows, width).astype(WIDE)
    fresh_update = shared[:, part : 2 * part].reshape(rows, width).astype(WIDE)
    fresh_sums = shared[:, 2 * part :].reshape(PLANE, 2, part, -1).transpose(1, 0, 2, 3).reshape(2, rows, -1).astype(WIDE)
    update = jnp.where(is_failed, fresh_update, adam(own_first, own_second, mean_grad))
    own_sums = jnp.stack([checksum(own_first), checksum(own_second)])
    checksums = jnp.where(is_failed, fresh_sums, own_sums)
    weight_checksums = checksum(restored_weight.astype(WIDE))
    return (key_out[None, None], outgoing[None, None], update[None, None], checksums[None, None], weight_checksums[None, None])


def solution(mesh):
    by_rows = P("replica", "section", "tensor", None)
    by_features = P("replica", "section", None, "tensor")
    return jax.shard_map(
        shards,
        mesh=mesh,
        in_specs=(by_features, by_features, by_rows, by_rows, by_rows, P(), P(), P()),
        out_specs=(by_features, by_features, by_rows, P("replica", "section", None, "tensor", None), by_rows),
        check_vma=False,
    )
```

```python
import jax
import jax.numpy as jnp
from jax import lax
from jax.experimental import pallas as pl
from jax.experimental.pallas import tpu as pltpu
from jax.sharding import PartitionSpec as P

SHORT = jnp.bfloat16
WIDE = jnp.float32
PLANE = 4
SPAN = 128


def from_behind(block, axis, distance):
    n = lax.axis_size(axis)
    return lax.ppermute(block, axis, [((i - distance) % n, i) for i in range(n)])


def swap(block, axis, bit):
    return lax.ppermute(block, axis, [(i, i ^ bit) for i in range(lax.axis_size(axis))])


def exchange_x(block):
    groups = [[0, 1, 2, 3], [4, 5, 6, 7]]
    return lax.all_to_all(block, "replica", 0, 0, axis_index_groups=groups, tiled=True)


def two_halves(value):
    high = value.astype(SHORT)
    return high, (value - high.astype(WIDE)).astype(SHORT)


def in_order(held, mine, bits):
    for bit in bits:
        split = held.reshape((held.shape[0] // (2 * bit), 2, bit) + held.shape[1:])
        held = jnp.where((mine & bit) != 0, split[:, ::-1], split).reshape(held.shape)
    return held


def doubled(held, mine, axis):
    bit = 4 >> axis
    came = swap(held, "tensor", bit)
    high = (mine & bit) != 0
    return jnp.stack([jnp.where(high, came, held), jnp.where(high, held, came)], axis=axis)


def gather_x(block):
    held = jnp.stack([block] + [swap(block, "replica", bit) for bit in (1, 2, 3)])
    return in_order(held, lax.axis_index("replica") & 3, (2, 1))


def broadcast_x(block):
    return exchange_x(jnp.broadcast_to(block[None], (PLANE,) + block.shape))


def tied(value, *after):
    return lax.optimization_barrier((value,) + after)[0]


def listed_bits(spans_ref, section):
    bits = jnp.int32(0)
    for j in range(spans_ref.shape[1]):
        bits = bits | lax.shift_left(jnp.int32(1), spans_ref[section, j])
    return bits


def pack_kernel(place_ref, spans_ref, weight_ref, primary_ref, second_ref):
    bits = listed_bits(spans_ref, place_ref[0])
    ahead = [jnp.int32(0), jnp.int32(0)]
    for n in range(weight_ref.shape[1] // SPAN):
        bit = lax.shift_right_logical(bits, n) & 1
        block = weight_ref[:, n * SPAN : (n + 1) * SPAN]

        def put(out_ref, slot, block=block):
            out_ref[:, pl.ds(pl.multiple_of(slot * SPAN, SPAN), SPAN)] = block

        pl.when(bit == 0)(lambda: put(primary_ref, ahead[0]))
        pl.when(bit == 1)(lambda: put(second_ref, ahead[1]))
        ahead = [ahead[0] + 1 - bit, ahead[1] + bit]


def pack(place, spans, weight, count):
    rows, width = weight.shape
    return pl.pallas_call(
        pack_kernel,
        out_shape=(
            jax.ShapeDtypeStruct((rows, width - count * SPAN), weight.dtype),
            jax.ShapeDtypeStruct((rows, count * SPAN), weight.dtype),
        ),
        in_specs=[pl.BlockSpec(memory_space=pltpu.SMEM)] * 2 + [pl.BlockSpec(memory_space=pltpu.VMEM)],
        out_specs=(pl.BlockSpec(memory_space=pltpu.VMEM),) * 2,
        name="pack",
    )(place, spans, weight)


def assemble_kernel(place_ref, spans_ref, own_ref, primary_ref, second_ref, grads_ref, sent_ref, restored_ref):
    bits = listed_bits(spans_ref, place_ref[0])
    here = place_ref[1] == 1
    rows = own_ref.shape[0]
    apart = sent_ref.shape[2] // SPAN
    last = (primary_ref.shape[1] // SPAN - 1, second_ref.shape[1] // SPAN - 1)
    ahead = [jnp.int32(0), jnp.int32(0)]
    for n in range(own_ref.shape[1] // SPAN):
        bit = lax.shift_right_logical(bits, n) & 1

        def taken(ref, slot, top):
            return ref[:, pl.ds(pl.multiple_of(jnp.minimum(slot, top) * SPAN, SPAN), SPAN)]

        fresh = jnp.where(bit == 1, taken(second_ref, ahead[1], last[1]), taken(primary_ref, ahead[0], last[0]))
        block = jnp.where(here, fresh, own_ref[:, n * SPAN : (n + 1) * SPAN])
        restored_ref[:, n * SPAN : (n + 1) * SPAN] = block
        inside = (n % apart) * SPAN
        sent_ref[n // apart, :rows, inside : inside + SPAN] = block
        ahead = [ahead[0] + 1 - bit, ahead[1] + bit]
    for t in range(sent_ref.shape[0]):
        total = grads_ref[0, t].astype(WIDE)
        for x in range(1, PLANE):
            total = total + grads_ref[x, t].astype(WIDE)
        sent_ref[t, rows:, :] = total.astype(SHORT)


def assemble(place, spans, own, primary, second, grads):
    rows, width = own.shape
    _, groups, part, cols = grads.shape
    return pl.pallas_call(
        assemble_kernel,
        out_shape=(
            jax.ShapeDtypeStruct((groups, rows + part, cols), SHORT),
            jax.ShapeDtypeStruct((rows, width), SHORT),
        ),
        in_specs=[pl.BlockSpec(memory_space=pltpu.SMEM)] * 2 + [pl.BlockSpec(memory_space=pltpu.VMEM)] * 4,
        out_specs=(pl.BlockSpec(memory_space=pltpu.VMEM),) * 2,
        name="assemble",
    )(place, spans, own, primary, second, grads)


def adam(first, second, grad):
    one = 0.9 * first + 0.1 * grad
    two = 0.95 * second + 0.05 * (grad * grad)
    return one / (jnp.sqrt(two) + 1e-08)


def shards(activations, key_grads, weight, first_moment, second_moment, probe_matrix, failed_replica, resend_spans):
    copies = lax.axis_size("replica")
    my_replica = lax.axis_index("replica")
    my_section = lax.axis_index("section")
    my_tensor = lax.axis_index("tensor")
    failed = failed_replica[my_section, my_tensor]
    my_spans = resend_spans[my_section]
    own_weight = weight[0, 0]
    own_first = first_moment[0, 0]
    own_second = second_moment[0, 0]
    rows, width = own_weight.shape
    nchunk = width // 128
    listed = jnp.any(my_spans[:, None] == jnp.arange(nchunk, dtype=jnp.int32)[None, :], axis=0)
    columns = jnp.repeat(listed, 128)[None, :]
    primary = jnp.bitwise_xor(failed, PLANE)
    second = jnp.bitwise_xor(failed, 1)
    chosen = jnp.where(columns, my_replica == second, my_replica == primary)
    is_failed = my_replica == failed
    part = rows // PLANE

    local = activations[0, 0]
    tokens, cols = local.shape
    incoming = from_behind(local, "section", 1)
    x = incoming.astype(WIDE)

    place = jnp.stack([my_section, is_failed.astype(jnp.int32)])
    to_primary, to_second = pack(place, resend_spans, own_weight, my_spans.shape[0])
    from_primary = swap(to_primary, "replica", PLANE)
    from_second = swap(to_second, "replica", 1)

    def masked(block):
        return jnp.where(chosen, block.astype(SHORT), 0).reshape(PLANE, 1, part, width)

    served = exchange_x(jnp.concatenate([masked(own_first), masked(own_second)], axis=1))
    served = jnp.sum(served.astype(WIDE), axis=0).astype(SHORT)

    squares = jnp.sum(x * x, axis=1).reshape(1, -1, 128)
    squares = lax.all_to_all(jnp.broadcast_to(squares, (8,) + squares.shape[1:]), "tensor", 0, 0, tiled=True)
    held = tied(key_grads[0, 0].T, to_primary)
    held = doubled(doubled(held, my_tensor, 0), my_tensor, 1)
    held, from_primary, from_second, squares, served = lax.optimization_barrier(
        (held, from_primary, from_second, squares, served)
    )
    fresh_moments = served + swap(served, "replica", PLANE)
    held = doubled(held, my_tensor, 2)
    kg_all = held.reshape(8 * rows, tokens)
    inverse_rms = 1.0 / jnp.sqrt(jnp.sum(squares, axis=0).reshape(tokens) / width + 1e-05)

    normed = (x * inverse_rms[:, None]).astype(SHORT)
    grad = lax.dot_general(kg_all, normed, (((1,), (0,)), ((), ())), preferred_element_type=WIDE).astype(SHORT)
    grad = grad.reshape(8, PLANE, part, cols).transpose(1, 0, 2, 3)
    grad, fresh_moments = lax.optimization_barrier((exchange_x(grad), fresh_moments))

    sent, restored_weight = assemble(place, resend_spans, own_weight, from_primary, from_second, grad)
    got = lax.all_to_all(sent, "tensor", 0, 0, tiled=True)
    weight_cols = got[:, :rows].reshape(8 * rows, cols)
    grad_rows = got[:, rows:].transpose(1, 0, 2).reshape(part, width)
    mean_rows = (grad_rows.astype(WIDE) + swap(grad_rows, "replica", PLANE).astype(WIDE)) / copies

    keys = lax.dot_general(weight_cols, normed, (((1,), (1,)), ((), ())), preferred_element_type=WIDE).astype(SHORT)
    feature = lax.dot_general(kg_all, weight_cols, (((0,), (0,)), ((), ())), preferred_element_type=WIDE)
    high, low = two_halves(jnp.sum(feature * x, axis=1))
    extra = jnp.concatenate([high[None], low[None], jnp.zeros((6, tokens), SHORT)], axis=0)
    sent = jnp.concatenate([keys.reshape(8, rows, tokens), jnp.broadcast_to(extra[None], (8, 8, tokens))], axis=1)
    got = jnp.sum(lax.all_to_all(sent, "tensor", 0, 0, tiled=True).astype(WIDE), axis=0)
    key_out = got[:rows].T.astype(SHORT)
    product = (got[rows] + got[rows + 1])[:, None]
    scale = inverse_rms[:, None]
    input_grad = scale * feature - scale * scale * scale * x * product / width
    outgoing = from_behind(input_grad.astype(SHORT), "section", -1)

    def checksum(source):
        shaped = source.reshape(-1, nchunk, 128)
        mixed = jnp.einsum("jnc,cp->jnp", shaped, probe_matrix, precision=lax.Precision.HIGHEST)
        return mixed.reshape(-1, nchunk * probe_matrix.shape[1])

    fresh = fresh_moments.astype(WIDE)
    fresh_update = adam(fresh[0], fresh[1], mean_rows).astype(SHORT)
    fresh_sums = checksum(fresh.reshape(2 * part, width)).astype(SHORT).reshape(2, width)
    shared = gather_x(jnp.concatenate([mean_rows.astype(SHORT), fresh_update, fresh_sums], axis=0))
    mean_grad = shared[:, :part].reshape(rows, width).astype(WIDE)
    fresh_update = shared[:, part : 2 * part].reshape(rows, width).astype(WIDE)
    fresh_sums = shared[:, 2 * part :].reshape(PLANE, 2, part, -1).transpose(1, 0, 2, 3).reshape(2, rows, -1).astype(WIDE)
    update = jnp.where(is_failed, fresh_update, adam(own_first, own_second, mean_grad))
    own_sums = jnp.stack([checksum(own_first), checksum(own_second)])
    checksums = jnp.where(is_failed, fresh_sums, own_sums)
    weight_checksums = checksum(restored_weight.astype(WIDE))
    return (key_out[None, None], outgoing[None, None], update[None, None], checksums[None, None], weight_checksums[None, None])


def solution(mesh):
    by_rows = P("replica", "section", "tensor", None)
    by_features = P("replica", "section", None, "tensor")
    return jax.shard_map(
        shards,
        mesh=mesh,
        in_specs=(by_features, by_features, by_rows, by_rows, by_rows, P(), P(), P()),
        out_specs=(by_features, by_features, by_rows, P("replica", "section", None, "tensor", None), by_rows),
        check_vma=False,
    )
```

```python
import jax
import jax.numpy as jnp
from jax import lax
from jax.experimental import pallas as pl
from jax.experimental.pallas import tpu as pltpu
from jax.sharding import PartitionSpec as P

SHORT = jnp.bfloat16
WIDE = jnp.float32
PLANE = 4
SPAN = 128


def from_behind(block, axis, distance):
    n = lax.axis_size(axis)
    return lax.ppermute(block, axis, [((i - distance) % n, i) for i in range(n)])


def swap(block, axis, bit):
    return lax.ppermute(block, axis, [(i, i ^ bit) for i in range(lax.axis_size(axis))])


def exchange_x(block):
    groups = [[0, 1, 2, 3], [4, 5, 6, 7]]
    return lax.all_to_all(block, "replica", 0, 0, axis_index_groups=groups, tiled=True)


def two_halves(value):
    high = value.astype(SHORT)
    return high, (value - high.astype(WIDE)).astype(SHORT)


def in_order(held, mine, bits):
    for bit in bits:
        split = held.reshape((held.shape[0] // (2 * bit), 2, bit) + held.shape[1:])
        held = jnp.where((mine & bit) != 0, split[:, ::-1], split).reshape(held.shape)
    return held


def doubled(held, mine, axis):
    bit = 4 >> axis
    came = swap(held, "tensor", bit)
    high = (mine & bit) != 0
    return jnp.stack([jnp.where(high, came, held), jnp.where(high, held, came)], axis=axis)


def gather_x(block):
    held = jnp.stack([block] + [swap(block, "replica", bit) for bit in (1, 2, 3)])
    return in_order(held, lax.axis_index("replica") & 3, (2, 1))


def broadcast_x(block):
    return exchange_x(jnp.broadcast_to(block[None], (PLANE,) + block.shape))


def tied(value, *after):
    return lax.optimization_barrier((value,) + after)[0]


def serve_kernel(failed_ref, spans_ref, weight_ref, first_ref, second_ref, out_ref):
    section = lax.axis_index("section")
    me = lax.axis_index("replica")
    failed = failed_ref[section, lax.axis_index("tensor")]
    is_primary = (failed ^ PLANE) == me
    is_second = (failed ^ 1) == me
    part = out_ref.shape[2]
    for n in range(weight_ref.shape[1] // SPAN):
        listed = spans_ref[section, 0] == n
        for j in range(1, spans_ref.shape[1]):
            listed = listed | (spans_ref[section, j] == n)
        take = (listed & is_second) | (jnp.logical_not(listed) & is_primary)
        here = pl.ds(n * SPAN, SPAN)
        for k, ref in enumerate((weight_ref, first_ref, second_ref)):
            for x in range(PLANE):
                block = ref[x * part : (x + 1) * part, here].astype(SHORT)
                out_ref[x, k, :, here] = jnp.where(take, block, jnp.zeros_like(block))


def serve(failed, spans, weight, first, second):
    rows, width = weight.shape
    return pl.pallas_call(
        serve_kernel,
        out_shape=jax.ShapeDtypeStruct((PLANE, 3, rows // PLANE, width), SHORT),
        in_specs=[pl.BlockSpec(memory_space=pltpu.SMEM)] * 2 + [pl.BlockSpec(memory_space=pltpu.VMEM)] * 3,
        out_specs=pl.BlockSpec(memory_space=pltpu.VMEM),
        name="serve",
    )(failed, spans, weight, first, second)


def assemble_kernel(failed_ref, own_ref, fresh0_ref, fresh1_ref, fresh2_ref, fresh3_ref, grads_ref, sent_ref, restored_ref):
    me = lax.axis_index("replica")
    here = failed_ref[lax.axis_index("section"), lax.axis_index("tensor")] == me
    rows = own_ref.shape[0]
    groups, _, cols = sent_ref.shape
    part = fresh0_ref.shape[0]
    for k, fresh_ref in enumerate((fresh0_ref, fresh1_ref, fresh2_ref, fresh3_ref)):
        at = pl.ds(pl.multiple_of(((me & 3) ^ k) * part, part), part)
        for t in range(groups):
            span = pl.ds(t * cols, cols)
            block = jnp.where(here, fresh_ref[:, span], own_ref[at, span])
            restored_ref[at, span] = block
            sent_ref[t, at, :] = block
    for t in range(groups):
        total = grads_ref[0, t].astype(WIDE)
        for x in range(1, PLANE):
            total = total + grads_ref[x, t].astype(WIDE)
        sent_ref[t, rows:, :] = total.astype(SHORT)


def assemble(failed, own, fresh, grads):
    rows, width = own.shape
    _, groups, part, cols = grads.shape
    return pl.pallas_call(
        assemble_kernel,
        out_shape=(
            jax.ShapeDtypeStruct((groups, rows + part, cols), SHORT),
            jax.ShapeDtypeStruct((rows, width), SHORT),
        ),
        in_specs=[pl.BlockSpec(memory_space=pltpu.SMEM)] + [pl.BlockSpec(memory_space=pltpu.VMEM)] * 6,
        out_specs=(pl.BlockSpec(memory_space=pltpu.VMEM),) * 2,
        name="assemble",
    )(failed, own, *fresh, grads)


def adam(first, second, grad):
    one = 0.9 * first + 0.1 * grad
    two = 0.95 * second + 0.05 * (grad * grad)
    return one / (jnp.sqrt(two) + 1e-08)


def shards(activations, key_grads, weight, first_moment, second_moment, probe_matrix, failed_replica, resend_spans):
    copies = lax.axis_size("replica")
    my_replica = lax.axis_index("replica")
    my_section = lax.axis_index("section")
    my_tensor = lax.axis_index("tensor")
    failed = failed_replica[my_section, my_tensor]
    my_spans = resend_spans[my_section]
    own_weight = weight[0, 0]
    own_first = first_moment[0, 0]
    own_second = second_moment[0, 0]
    rows, width = own_weight.shape
    nchunk = width // 128
    listed = jnp.any(my_spans[:, None] == jnp.arange(nchunk, dtype=jnp.int32)[None, :], axis=0)
    columns = jnp.repeat(listed, 128)[None, :]
    primary = jnp.bitwise_xor(failed, PLANE)
    second = jnp.bitwise_xor(failed, 1)
    chosen = jnp.where(columns, my_replica == second, my_replica == primary)
    is_failed = my_replica == failed
    part = rows // PLANE

    local = activations[0, 0]
    tokens, cols = local.shape
    incoming = from_behind(local, "section", 1)
    x = incoming.astype(WIDE)

    mask = serve(failed_replica, resend_spans, own_weight, own_first, own_second)
    served = jnp.sum(exchange_x(mask).astype(WIDE), axis=0).astype(SHORT)

    squares = jnp.sum(x * x, axis=1).reshape(1, -1, 128)
    squares = lax.all_to_all(jnp.broadcast_to(squares, (8,) + squares.shape[1:]), "tensor", 0, 0, tiled=True)
    held = tied(key_grads[0, 0].T, mask)
    held = doubled(doubled(held, my_tensor, 0), my_tensor, 1)
    held, served = lax.optimization_barrier((held, served))
    fresh_weight = served[0] + swap(served[0], "replica", PLANE)
    held = doubled(held, my_tensor, 2)
    held, fresh_weight, squares = lax.optimization_barrier((held, fresh_weight, squares))
    served_moments = tied(served[1:], fresh_weight)
    fresh_moments = served_moments + swap(served_moments, "replica", PLANE)
    kg_all = held.reshape(8 * rows, tokens)
    inverse_rms = 1.0 / jnp.sqrt(jnp.sum(squares, axis=0).reshape(tokens) / width + 1e-05)
    fresh_weight = [fresh_weight] + [swap(fresh_weight, "replica", bit) for bit in (1, 2, 3)]

    normed = (x * inverse_rms[:, None]).astype(SHORT)
    grad = lax.dot_general(kg_all, normed, (((1,), (0,)), ((), ())), preferred_element_type=WIDE).astype(SHORT)
    grad = grad.reshape(8, PLANE, part, cols).transpose(1, 0, 2, 3)
    grad, fresh_moments = lax.optimization_barrier((exchange_x(grad), fresh_moments))

    sent, restored_weight = assemble(failed_replica, own_weight, fresh_weight, grad)
    got = lax.all_to_all(sent, "tensor", 0, 0, tiled=True)
    weight_cols = got[:, :rows].reshape(8 * rows, cols)
    grad_rows = got[:, rows:].transpose(1, 0, 2).reshape(part, width)
    mean_rows = (grad_rows.astype(WIDE) + swap(grad_rows, "replica", PLANE).astype(WIDE)) / copies

    keys = lax.dot_general(weight_cols, normed, (((1,), (1,)), ((), ())), preferred_element_type=WIDE).astype(SHORT)
    feature = lax.dot_general(kg_all, weight_cols, (((0,), (0,)), ((), ())), preferred_element_type=WIDE)
    product = jnp.sum(feature * x, axis=1).reshape(-1, 128)
    for bit in (1, 2, 4):
        product = product + swap(product, "tensor", bit)
    product = product.reshape(tokens, 1)
    scale = inverse_rms[:, None]
    input_grad = scale * feature - scale * scale * scale * x * product / width
    outgoing = from_behind(input_grad.astype(SHORT), "section", -1)
    got = lax.all_to_all(keys.reshape(8, rows, tokens), "tensor", 0, 0, tiled=True)
    key_out = jnp.sum(got.astype(WIDE), axis=0).T.astype(SHORT)

    def checksum(source):
        shaped = source.reshape(-1, nchunk, 128)
        mixed = jnp.einsum("jnc,cp->jnp", shaped, probe_matrix, precision=lax.Precision.HIGHEST)
        return mixed.reshape(-1, nchunk * probe_matrix.shape[1])

    fresh = fresh_moments.astype(WIDE)
    fresh_update = adam(fresh[0], fresh[1], mean_rows).astype(SHORT)
    fresh_sums = checksum(fresh.reshape(2 * part, width)).astype(SHORT).reshape(2, width)
    shared = gather_x(jnp.concatenate([mean_rows.astype(SHORT), fresh_update, fresh_sums], axis=0))
    mean_grad = shared[:, :part].reshape(rows, width).astype(WIDE)
    fresh_update = shared[:, part : 2 * part].reshape(rows, width).astype(WIDE)
    fresh_sums = shared[:, 2 * part :].reshape(PLANE, 2, part, -1).transpose(1, 0, 2, 3).reshape(2, rows, -1).astype(WIDE)
    update = jnp.where(is_failed, fresh_update, adam(own_first, own_second, mean_grad))
    own_sums = jnp.stack([checksum(own_first), checksum(own_second)])
    checksums = jnp.where(is_failed, fresh_sums, own_sums)
    weight_checksums = checksum(restored_weight.astype(WIDE))
    return (key_out[None, None], outgoing[None, None], update[None, None], checksums[None, None], weight_checksums[None, None])


def solution(mesh):
    by_rows = P("replica", "section", "tensor", None)
    by_features = P("replica", "section", None, "tensor")
    return jax.shard_map(
        shards,
        mesh=mesh,
        in_specs=(by_features, by_features, by_rows, by_rows, by_rows, P(), P(), P()),
        out_specs=(by_features, by_features, by_rows, P("replica", "section", None, "tensor", None), by_rows),
        check_vma=False,
    )
```

```python
import jax
import jax.numpy as jnp
from jax import lax
from jax.experimental import pallas as pl
from jax.experimental.pallas import tpu as pltpu
from jax.sharding import PartitionSpec as P

SHORT = jnp.bfloat16
WIDE = jnp.float32
PLANE = 4
SPAN = 128


def from_behind(block, axis, distance):
    n = lax.axis_size(axis)
    return lax.ppermute(block, axis, [((i - distance) % n, i) for i in range(n)])


def swap(block, axis, bit):
    return lax.ppermute(block, axis, [(i, i ^ bit) for i in range(lax.axis_size(axis))])


def exchange_x(block):
    groups = [[0, 1, 2, 3], [4, 5, 6, 7]]
    return lax.all_to_all(block, "replica", 0, 0, axis_index_groups=groups, tiled=True)


def two_halves(value):
    high = value.astype(SHORT)
    return high, (value - high.astype(WIDE)).astype(SHORT)


def in_order(held, mine, bits):
    for bit in bits:
        split = held.reshape((held.shape[0] // (2 * bit), 2, bit) + held.shape[1:])
        held = jnp.where((mine & bit) != 0, split[:, ::-1], split).reshape(held.shape)
    return held


def doubled(held, mine, axis):
    bit = 4 >> axis
    came = swap(held, "tensor", bit)
    high = (mine & bit) != 0
    return jnp.stack([jnp.where(high, came, held), jnp.where(high, held, came)], axis=axis)


def gather_x(block):
    held = jnp.stack([block] + [swap(block, "replica", bit) for bit in (1, 2, 3)])
    return in_order(held, lax.axis_index("replica") & 3, (2, 1))


def broadcast_x(block):
    return exchange_x(jnp.broadcast_to(block[None], (PLANE,) + block.shape))


def tied(value, *after):
    return lax.optimization_barrier((value,) + after)[0]


def serve_kernel(failed_ref, spans_ref, weight_ref, first_ref, second_ref, weight_out_ref, moments_out_ref):
    section = lax.axis_index("section")
    me = lax.axis_index("replica")
    failed = failed_ref[section, lax.axis_index("tensor")]
    is_primary = (failed ^ PLANE) == me
    is_second = (failed ^ 1) == me
    part = weight_out_ref.shape[1]
    for n in range(weight_ref.shape[1] // SPAN):
        listed = spans_ref[section, 0] == n
        for j in range(1, spans_ref.shape[1]):
            listed = listed | (spans_ref[section, j] == n)
        take = (listed & is_second) | (jnp.logical_not(listed) & is_primary)
        here = pl.ds(n * SPAN, SPAN)
        for x in range(PLANE):
            at = pl.ds(x * part, part)
            block = weight_ref[at, here]
            weight_out_ref[x, :, here] = jnp.where(take, block, jnp.zeros_like(block))
            for k, ref in enumerate((first_ref, second_ref)):
                block = ref[at, here].astype(SHORT)
                moments_out_ref[x, k, :, here] = jnp.where(take, block, jnp.zeros_like(block))


def serve(failed, spans, weight, first, second):
    rows, width = weight.shape
    return pl.pallas_call(
        serve_kernel,
        out_shape=(
            jax.ShapeDtypeStruct((PLANE, rows // PLANE, width), SHORT),
            jax.ShapeDtypeStruct((PLANE, 2, rows // PLANE, width), SHORT),
        ),
        in_specs=[pl.BlockSpec(memory_space=pltpu.SMEM)] * 2 + [pl.BlockSpec(memory_space=pltpu.VMEM)] * 3,
        out_specs=(pl.BlockSpec(memory_space=pltpu.VMEM),) * 2,
        name="serve",
    )(failed, spans, weight, first, second)


def assemble_kernel(failed_ref, own_ref, fresh0_ref, fresh1_ref, fresh2_ref, fresh3_ref, grads_ref, sent_ref, restored_ref):
    me = lax.axis_index("replica")
    here = failed_ref[lax.axis_index("section"), lax.axis_index("tensor")] == me
    rows = own_ref.shape[0]
    groups, _, cols = sent_ref.shape
    part = fresh0_ref.shape[0]
    for k, fresh_ref in enumerate((fresh0_ref, fresh1_ref, fresh2_ref, fresh3_ref)):
        at = pl.ds(pl.multiple_of(((me & 3) ^ k) * part, part), part)
        for t in range(groups):
            span = pl.ds(t * cols, cols)
            block = jnp.where(here, fresh_ref[:, span], own_ref[at, span])
            restored_ref[at, span] = block
            sent_ref[t, at, :] = block
    for t in range(groups):
        total = grads_ref[0, t].astype(WIDE)
        for x in range(1, PLANE):
            total = total + grads_ref[x, t].astype(WIDE)
        sent_ref[t, rows:, :] = total.astype(SHORT)


def assemble(failed, own, fresh, grads):
    rows, width = own.shape
    _, groups, part, cols = grads.shape
    return pl.pallas_call(
        assemble_kernel,
        out_shape=(
            jax.ShapeDtypeStruct((groups, rows + part, cols), SHORT),
            jax.ShapeDtypeStruct((rows, width), SHORT),
        ),
        in_specs=[pl.BlockSpec(memory_space=pltpu.SMEM)] + [pl.BlockSpec(memory_space=pltpu.VMEM)] * 6,
        out_specs=(pl.BlockSpec(memory_space=pltpu.VMEM),) * 2,
        name="assemble",
    )(failed, own, *fresh, grads)


def adam(first, second, grad):
    one = 0.9 * first + 0.1 * grad
    two = 0.95 * second + 0.05 * (grad * grad)
    return one / (jnp.sqrt(two) + 1e-08)


def shards(activations, key_grads, weight, first_moment, second_moment, probe_matrix, failed_replica, resend_spans):
    copies = lax.axis_size("replica")
    my_replica = lax.axis_index("replica")
    my_section = lax.axis_index("section")
    my_tensor = lax.axis_index("tensor")
    failed = failed_replica[my_section, my_tensor]
    my_spans = resend_spans[my_section]
    own_weight = weight[0, 0]
    own_first = first_moment[0, 0]
    own_second = second_moment[0, 0]
    rows, width = own_weight.shape
    nchunk = width // 128
    listed = jnp.any(my_spans[:, None] == jnp.arange(nchunk, dtype=jnp.int32)[None, :], axis=0)
    columns = jnp.repeat(listed, 128)[None, :]
    primary = jnp.bitwise_xor(failed, PLANE)
    second = jnp.bitwise_xor(failed, 1)
    chosen = jnp.where(columns, my_replica == second, my_replica == primary)
    is_failed = my_replica == failed
    part = rows // PLANE

    local = activations[0, 0]
    tokens, cols = local.shape
    incoming = from_behind(local, "section", 1)
    x = incoming.astype(WIDE)

    def summed(parts):
        return jnp.sum(parts.astype(WIDE), axis=0).astype(SHORT)

    mask_weight, mask_moments = serve(failed_replica, resend_spans, own_weight, own_first, own_second)
    served_weight = summed(exchange_x(mask_weight))
    served_moments = summed(exchange_x(tied(mask_moments, served_weight)))

    squares = jnp.sum(x * x, axis=1).reshape(1, -1, 128)
    squares = lax.all_to_all(jnp.broadcast_to(squares, (8,) + squares.shape[1:]), "tensor", 0, 0, tiled=True)
    held = doubled(tied(key_grads[0, 0].T, mask_weight), my_tensor, 0)
    held, served_weight = lax.optimization_barrier((held, served_weight))
    fresh_weight = served_weight + swap(served_weight, "replica", PLANE)
    held = doubled(held, my_tensor, 1)
    held, fresh_weight, served_moments = lax.optimization_barrier((held, fresh_weight, served_moments))
    fresh_moments = served_moments + swap(served_moments, "replica", PLANE)
    fresh_weight = [fresh_weight] + [swap(fresh_weight, "replica", bit) for bit in (1, 2, 3)]
    held = doubled(held, my_tensor, 2)
    held, fresh_weight, squares = lax.optimization_barrier((held, fresh_weight, squares))
    kg_all = held.reshape(8 * rows, tokens)
    inverse_rms = 1.0 / jnp.sqrt(jnp.sum(squares, axis=0).reshape(tokens) / width + 1e-05)

    normed = (x * inverse_rms[:, None]).astype(SHORT)
    grad = lax.dot_general(kg_all, normed, (((1,), (0,)), ((), ())), preferred_element_type=WIDE).astype(SHORT)
    grad = grad.reshape(8, PLANE, part, cols).transpose(1, 0, 2, 3)
    grad, fresh_moments = lax.optimization_barrier((exchange_x(grad), fresh_moments))

    sent, restored_weight = assemble(failed_replica, own_weight, fresh_weight, grad)
    got = lax.all_to_all(sent, "tensor", 0, 0, tiled=True)
    weight_cols = got[:, :rows].reshape(8 * rows, cols)
    grad_rows = got[:, rows:].transpose(1, 0, 2).reshape(part, width)
    mean_rows = (grad_rows.astype(WIDE) + swap(grad_rows, "replica", PLANE).astype(WIDE)) / copies

    keys = lax.dot_general(weight_cols, normed, (((1,), (1,)), ((), ())), preferred_element_type=WIDE).astype(SHORT)
    feature = lax.dot_general(kg_all, weight_cols, (((0,), (0,)), ((), ())), preferred_element_type=WIDE)
    product = jnp.sum(feature * x, axis=1).reshape(-1, 128)
    for bit in (1, 2, 4):
        product = product + swap(product, "tensor", bit)
    product = product.reshape(tokens, 1)
    scale = inverse_rms[:, None]
    input_grad = scale * feature - scale * scale * scale * x * product / width
    outgoing = from_behind(input_grad.astype(SHORT), "section", -1)
    got = lax.all_to_all(keys.reshape(8, rows, tokens), "tensor", 0, 0, tiled=True)
    key_out = jnp.sum(got.astype(WIDE), axis=0).T.astype(SHORT)

    def checksum(source):
        shaped = source.reshape(-1, nchunk, 128)
        mixed = jnp.einsum("jnc,cp->jnp", shaped, probe_matrix, precision=lax.Precision.HIGHEST)
        return mixed.reshape(-1, nchunk * probe_matrix.shape[1])

    fresh = fresh_moments.astype(WIDE)
    fresh_update = adam(fresh[0], fresh[1], mean_rows).astype(SHORT)
    fresh_sums = checksum(fresh.reshape(2 * part, width)).astype(SHORT).reshape(2, width)
    shared = gather_x(jnp.concatenate([mean_rows.astype(SHORT), fresh_update, fresh_sums], axis=0))
    mean_grad = shared[:, :part].reshape(rows, width).astype(WIDE)
    fresh_update = shared[:, part : 2 * part].reshape(rows, width).astype(WIDE)
    fresh_sums = shared[:, 2 * part :].reshape(PLANE, 2, part, -1).transpose(1, 0, 2, 3).reshape(2, rows, -1).astype(WIDE)
    update = jnp.where(is_failed, fresh_update, adam(own_first, own_second, mean_grad))
    own_sums = jnp.stack([checksum(own_first), checksum(own_second)])
    checksums = jnp.where(is_failed, fresh_sums, own_sums)
    weight_checksums = checksum(restored_weight.astype(WIDE))
    return (key_out[None, None], outgoing[None, None], update[None, None], checksums[None, None], weight_checksums[None, None])


def solution(mesh):
    by_rows = P("replica", "section", "tensor", None)
    by_features = P("replica", "section", None, "tensor")
    return jax.shard_map(
        shards,
        mesh=mesh,
        in_specs=(by_features, by_features, by_rows, by_rows, by_rows, P(), P(), P()),
        out_specs=(by_features, by_features, by_rows, P("replica", "section", None, "tensor", None), by_rows),
        check_vma=False,
    )
```

```python
import jax
import jax.numpy as jnp
from jax import lax
from jax.experimental import pallas as pl
from jax.experimental.pallas import tpu as pltpu
from jax.sharding import PartitionSpec as P

SHORT = jnp.bfloat16
WIDE = jnp.float32
PLANE = 4
SPAN = 128


def from_behind(block, axis, distance):
    n = lax.axis_size(axis)
    return lax.ppermute(block, axis, [((i - distance) % n, i) for i in range(n)])


def swap(block, axis, bit):
    return lax.ppermute(block, axis, [(i, i ^ bit) for i in range(lax.axis_size(axis))])


def exchange_x(block):
    groups = [[0, 1, 2, 3], [4, 5, 6, 7]]
    return lax.all_to_all(block, "replica", 0, 0, axis_index_groups=groups, tiled=True)


def two_halves(value):
    high = value.astype(SHORT)
    return high, (value - high.astype(WIDE)).astype(SHORT)


def in_order(held, mine, bits):
    for bit in bits:
        split = held.reshape((held.shape[0] // (2 * bit), 2, bit) + held.shape[1:])
        held = jnp.where((mine & bit) != 0, split[:, ::-1], split).reshape(held.shape)
    return held


def doubled(held, mine, axis):
    bit = 4 >> axis
    came = swap(held, "tensor", bit)
    high = (mine & bit) != 0
    return jnp.stack([jnp.where(high, came, held), jnp.where(high, held, came)], axis=axis)


def gather_x(block):
    held = jnp.stack([block] + [swap(block, "replica", bit) for bit in (1, 2, 3)])
    return in_order(held, lax.axis_index("replica") & 3, (2, 1))


def broadcast_x(block):
    return exchange_x(jnp.broadcast_to(block[None], (PLANE,) + block.shape))


def tied(value, *after):
    return lax.optimization_barrier((value,) + after)[0]


def serve_kernel(failed_ref, spans_ref, weight_ref, first_ref, second_ref, out_ref):
    section = lax.axis_index("section")
    me = lax.axis_index("replica")
    failed = failed_ref[section, lax.axis_index("tensor")]
    is_primary = (failed ^ PLANE) == me
    is_second = (failed ^ 1) == me
    part = out_ref.shape[2]
    for n in range(weight_ref.shape[1] // SPAN):
        listed = spans_ref[section, 0] == n
        for j in range(1, spans_ref.shape[1]):
            listed = listed | (spans_ref[section, j] == n)
        take = (listed & is_second) | (jnp.logical_not(listed) & is_primary)
        here = pl.ds(n * SPAN, SPAN)
        for k, ref in enumerate((weight_ref, first_ref, second_ref)):
            for x in range(PLANE):
                block = ref[x * part : (x + 1) * part, here].astype(SHORT)
                out_ref[x, k, :, here] = jnp.where(take, block, jnp.zeros_like(block))


def serve(failed, spans, weight, first, second):
    rows, width = weight.shape
    return pl.pallas_call(
        serve_kernel,
        out_shape=jax.ShapeDtypeStruct((PLANE, 3, rows // PLANE, width), SHORT),
        in_specs=[pl.BlockSpec(memory_space=pltpu.SMEM)] * 2 + [pl.BlockSpec(memory_space=pltpu.VMEM)] * 3,
        out_specs=pl.BlockSpec(memory_space=pltpu.VMEM),
        name="serve",
    )(failed, spans, weight, first, second)


def assemble_kernel(failed_ref, own_ref, fresh0_ref, fresh1_ref, fresh2_ref, fresh3_ref, grads_ref, sent_ref, restored_ref):
    me = lax.axis_index("replica")
    here = failed_ref[lax.axis_index("section"), lax.axis_index("tensor")] == me
    rows = own_ref.shape[0]
    groups, _, cols = sent_ref.shape
    part = fresh0_ref.shape[0]
    for k, fresh_ref in enumerate((fresh0_ref, fresh1_ref, fresh2_ref, fresh3_ref)):
        at = pl.ds(pl.multiple_of(((me & 3) ^ k) * part, part), part)
        for t in range(groups):
            span = pl.ds(t * cols, cols)
            block = jnp.where(here, fresh_ref[:, span], own_ref[at, span])
            restored_ref[at, span] = block
            sent_ref[t, at, :] = block
    for t in range(groups):
        total = grads_ref[0, t].astype(WIDE)
        for x in range(1, PLANE):
            total = total + grads_ref[x, t].astype(WIDE)
        sent_ref[t, rows:, :] = total.astype(SHORT)


def assemble(failed, own, fresh, grads):
    rows, width = own.shape
    _, groups, part, cols = grads.shape
    return pl.pallas_call(
        assemble_kernel,
        out_shape=(
            jax.ShapeDtypeStruct((groups, rows + part, cols), SHORT),
            jax.ShapeDtypeStruct((rows, width), SHORT),
        ),
        in_specs=[pl.BlockSpec(memory_space=pltpu.SMEM)] + [pl.BlockSpec(memory_space=pltpu.VMEM)] * 6,
        out_specs=(pl.BlockSpec(memory_space=pltpu.VMEM),) * 2,
        name="assemble",
    )(failed, own, *fresh, grads)


def adam(first, second, grad):
    one = 0.9 * first + 0.1 * grad
    two = 0.95 * second + 0.05 * (grad * grad)
    return one / (jnp.sqrt(two) + 1e-08)


def shards(activations, key_grads, weight, first_moment, second_moment, probe_matrix, failed_replica, resend_spans):
    copies = lax.axis_size("replica")
    my_replica = lax.axis_index("replica")
    my_section = lax.axis_index("section")
    my_tensor = lax.axis_index("tensor")
    failed = failed_replica[my_section, my_tensor]
    my_spans = resend_spans[my_section]
    own_weight = weight[0, 0]
    own_first = first_moment[0, 0]
    own_second = second_moment[0, 0]
    rows, width = own_weight.shape
    nchunk = width // 128
    listed = jnp.any(my_spans[:, None] == jnp.arange(nchunk, dtype=jnp.int32)[None, :], axis=0)
    columns = jnp.repeat(listed, 128)[None, :]
    primary = jnp.bitwise_xor(failed, PLANE)
    second = jnp.bitwise_xor(failed, 1)
    chosen = jnp.where(columns, my_replica == second, my_replica == primary)
    is_failed = my_replica == failed
    part = rows // PLANE

    local = activations[0, 0]
    tokens, cols = local.shape
    incoming = from_behind(local, "section", 1)
    x = incoming.astype(WIDE)

    mask = serve(failed_replica, resend_spans, own_weight, own_first, own_second)
    served = jnp.sum(exchange_x(mask).astype(WIDE), axis=0).astype(SHORT)

    squares = jnp.sum(x * x, axis=1).reshape(1, -1, 128)
    squares = lax.all_to_all(jnp.broadcast_to(squares, (8,) + squares.shape[1:]), "tensor", 0, 0, tiled=True)
    held = tied(key_grads[0, 0].T, mask)
    held = doubled(doubled(held, my_tensor, 0), my_tensor, 1)
    held, served = lax.optimization_barrier((held, served))
    fresh_weight = served[0] + swap(served[0], "replica", PLANE)
    held = doubled(held, my_tensor, 2)
    held, fresh_weight, squares = lax.optimization_barrier((held, fresh_weight, squares))
    kg_all = held.reshape(8 * rows, tokens)
    inverse_rms = 1.0 / jnp.sqrt(jnp.sum(squares, axis=0).reshape(tokens) / width + 1e-05)
    fresh_weight = [fresh_weight] + [swap(fresh_weight, "replica", bit) for bit in (1, 2, 3)]

    normed = (x * inverse_rms[:, None]).astype(SHORT)
    grad = lax.dot_general(kg_all, normed, (((1,), (0,)), ((), ())), preferred_element_type=WIDE).astype(SHORT)
    grad = grad.reshape(8, PLANE, part, cols).transpose(1, 0, 2, 3)
    grad = exchange_x(grad)

    sent, restored_weight = assemble(failed_replica, own_weight, fresh_weight, grad)
    got = lax.all_to_all(sent, "tensor", 0, 0, tiled=True)
    weight_cols = got[:, :rows].reshape(8 * rows, cols)
    grad_rows = got[:, rows:].transpose(1, 0, 2).reshape(part, width)
    mean_rows = (grad_rows.astype(WIDE) + swap(grad_rows, "replica", PLANE).astype(WIDE)) / copies

    keys = lax.dot_general(weight_cols, normed, (((1,), (1,)), ((), ())), preferred_element_type=WIDE).astype(SHORT)
    feature = lax.dot_general(kg_all, weight_cols, (((0,), (0,)), ((), ())), preferred_element_type=WIDE)
    product = jnp.sum(feature * x, axis=1).reshape(-1, 128)
    product = product + swap(product, "tensor", 1)
    product, mean_rows = lax.optimization_barrier((product, mean_rows))
    for bit in (2, 4):
        product = product + swap(product, "tensor", bit)
    product = product.reshape(tokens, 1)
    scale = inverse_rms[:, None]
    input_grad = scale * feature - scale * scale * scale * x * product / width
    outgoing = from_behind(input_grad.astype(SHORT), "section", -1)
    got = lax.all_to_all(keys.reshape(8, rows, tokens), "tensor", 0, 0, tiled=True)
    key_out = jnp.sum(got.astype(WIDE), axis=0).T.astype(SHORT)

    def checksum(source):
        shaped = source.reshape(-1, nchunk, 128)
        mixed = jnp.einsum("jnc,cp->jnp", shaped, probe_matrix, precision=lax.Precision.HIGHEST)
        return mixed.reshape(-1, nchunk * probe_matrix.shape[1])

    served_moments = served[1:].astype(WIDE)
    served_update = adam(served_moments[0], served_moments[1], mean_rows).astype(SHORT)
    served_sums = checksum(served_moments.reshape(2 * part, width)).astype(SHORT).reshape(2, width)
    mine = jnp.concatenate([served_update, served_sums], axis=0)
    other = swap(mine, "replica", PLANE)
    fresh_update = jnp.where(columns, mine[:part], other[:part])
    fresh_sums = mine[part:] + other[part:]
    shared = jnp.concatenate([mean_rows.astype(SHORT), fresh_update, fresh_sums], axis=0)
    shared, key_out = lax.optimization_barrier((shared, key_out))
    shared = gather_x(shared)
    mean_grad = shared[:, :part].reshape(rows, width).astype(WIDE)
    fresh_update = shared[:, part : 2 * part].reshape(rows, width).astype(WIDE)
    fresh_sums = shared[:, 2 * part :].reshape(PLANE, 2, part, -1).transpose(1, 0, 2, 3).reshape(2, rows, -1).astype(WIDE)
    update = jnp.where(is_failed, fresh_update, adam(own_first, own_second, mean_grad))
    own_sums = jnp.stack([checksum(own_first), checksum(own_second)])
    checksums = jnp.where(is_failed, fresh_sums, own_sums)
    weight_checksums = checksum(restored_weight.astype(WIDE))
    return (key_out[None, None], outgoing[None, None], update[None, None], checksums[None, None], weight_checksums[None, None])


def solution(mesh):
    by_rows = P("replica", "section", "tensor", None)
    by_features = P("replica", "section", None, "tensor")
    return jax.shard_map(
        shards,
        mesh=mesh,
        in_specs=(by_features, by_features, by_rows, by_rows, by_rows, P(), P(), P()),
        out_specs=(by_features, by_features, by_rows, P("replica", "section", None, "tensor", None), by_rows),
        check_vma=False,
    )
```

```python
import jax
import jax.numpy as jnp
from jax import lax
from jax.experimental import pallas as pl
from jax.experimental.pallas import tpu as pltpu
from jax.sharding import PartitionSpec as P

SHORT = jnp.bfloat16
WIDE = jnp.float32
PLANE = 4
SPAN = 128


def from_behind(block, axis, distance):
    n = lax.axis_size(axis)
    return lax.ppermute(block, axis, [((i - distance) % n, i) for i in range(n)])


def swap(block, axis, bit):
    return lax.ppermute(block, axis, [(i, i ^ bit) for i in range(lax.axis_size(axis))])


def exchange_x(block):
    groups = [[0, 1, 2, 3], [4, 5, 6, 7]]
    return lax.all_to_all(block, "replica", 0, 0, axis_index_groups=groups, tiled=True)


def two_halves(value):
    high = value.astype(SHORT)
    return high, (value - high.astype(WIDE)).astype(SHORT)


def in_order(held, mine, bits):
    for bit in bits:
        split = held.reshape((held.shape[0] // (2 * bit), 2, bit) + held.shape[1:])
        held = jnp.where((mine & bit) != 0, split[:, ::-1], split).reshape(held.shape)
    return held


def doubled(held, mine, axis):
    bit = 4 >> axis
    came = swap(held, "tensor", bit)
    high = (mine & bit) != 0
    return jnp.stack([jnp.where(high, came, held), jnp.where(high, held, came)], axis=axis)


def gather_x(block):
    held = jnp.stack([block] + [swap(block, "replica", bit) for bit in (1, 2, 3)])
    return in_order(held, lax.axis_index("replica") & 3, (2, 1))


def broadcast_x(block):
    return exchange_x(jnp.broadcast_to(block[None], (PLANE,) + block.shape))


def tied(value, *after):
    return lax.optimization_barrier((value,) + after)[0]


def serve_kernel(failed_ref, spans_ref, weight_ref, first_ref, second_ref, out_ref):
    section = lax.axis_index("section")
    me = lax.axis_index("replica")
    failed = failed_ref[section, lax.axis_index("tensor")]
    is_primary = (failed ^ PLANE) == me
    is_second = (failed ^ 1) == me
    part = out_ref.shape[2]
    for n in range(weight_ref.shape[1] // SPAN):
        listed = spans_ref[section, 0] == n
        for j in range(1, spans_ref.shape[1]):
            listed = listed | (spans_ref[section, j] == n)
        take = (listed & is_second) | (jnp.logical_not(listed) & is_primary)
        here = pl.ds(n * SPAN, SPAN)
        for k, ref in enumerate((weight_ref, first_ref, second_ref)):
            for x in range(PLANE):
                block = ref[x * part : (x + 1) * part, here].astype(SHORT)
                out_ref[x, k, :, here] = jnp.where(take, block, jnp.zeros_like(block))


def serve(failed, spans, weight, first, second):
    rows, width = weight.shape
    return pl.pallas_call(
        serve_kernel,
        out_shape=jax.ShapeDtypeStruct((PLANE, 3, rows // PLANE, width), SHORT),
        in_specs=[pl.BlockSpec(memory_space=pltpu.SMEM)] * 2 + [pl.BlockSpec(memory_space=pltpu.VMEM)] * 3,
        out_specs=pl.BlockSpec(memory_space=pltpu.VMEM),
        name="serve",
    )(failed, spans, weight, first, second)


def assemble_kernel(failed_ref, own_ref, fresh0_ref, fresh1_ref, fresh2_ref, fresh3_ref, sent_ref, restored_ref):
    me = lax.axis_index("replica")
    here = failed_ref[lax.axis_index("section"), lax.axis_index("tensor")] == me
    groups, _, cols = sent_ref.shape
    part = fresh0_ref.shape[0]
    for k, fresh_ref in enumerate((fresh0_ref, fresh1_ref, fresh2_ref, fresh3_ref)):
        at = pl.ds(pl.multiple_of(((me & 3) ^ k) * part, part), part)
        for t in range(groups):
            span = pl.ds(t * cols, cols)
            block = jnp.where(here, fresh_ref[:, span], own_ref[at, span])
            restored_ref[at, span] = block
            sent_ref[t, at, :] = block


def assemble(failed, own, fresh):
    rows, width = own.shape
    groups = 8
    return pl.pallas_call(
        assemble_kernel,
        out_shape=(
            jax.ShapeDtypeStruct((groups, rows, width // groups), SHORT),
            jax.ShapeDtypeStruct((rows, width), SHORT),
        ),
        in_specs=[pl.BlockSpec(memory_space=pltpu.SMEM)] + [pl.BlockSpec(memory_space=pltpu.VMEM)] * 5,
        out_specs=(pl.BlockSpec(memory_space=pltpu.VMEM),) * 2,
        name="assemble",
    )(failed, own, *fresh)


def adam(first, second, grad):
    one = 0.9 * first + 0.1 * grad
    two = 0.95 * second + 0.05 * (grad * grad)
    return one / (jnp.sqrt(two) + 1e-08)


def shards(activations, key_grads, weight, first_moment, second_moment, probe_matrix, failed_replica, resend_spans):
    copies = lax.axis_size("replica")
    my_replica = lax.axis_index("replica")
    my_section = lax.axis_index("section")
    my_tensor = lax.axis_index("tensor")
    failed = failed_replica[my_section, my_tensor]
    my_spans = resend_spans[my_section]
    own_weight = weight[0, 0]
    own_first = first_moment[0, 0]
    own_second = second_moment[0, 0]
    rows, width = own_weight.shape
    nchunk = width // 128
    listed = jnp.any(my_spans[:, None] == jnp.arange(nchunk, dtype=jnp.int32)[None, :], axis=0)
    columns = jnp.repeat(listed, 128)[None, :]
    primary = jnp.bitwise_xor(failed, PLANE)
    second = jnp.bitwise_xor(failed, 1)
    chosen = jnp.where(columns, my_replica == second, my_replica == primary)
    is_failed = my_replica == failed
    part = rows // PLANE

    local = activations[0, 0]
    tokens, cols = local.shape
    incoming = from_behind(local, "section", 1)
    x = incoming.astype(WIDE)

    mask = serve(failed_replica, resend_spans, own_weight, own_first, own_second)
    served = jnp.sum(exchange_x(mask).astype(WIDE), axis=0).astype(SHORT)

    squares = jnp.sum(x * x, axis=1).reshape(1, -1, 128)
    squares = lax.all_to_all(jnp.broadcast_to(squares, (8,) + squares.shape[1:]), "tensor", 0, 0, tiled=True)
    held = tied(key_grads[0, 0].T, mask)
    held = doubled(doubled(held, my_tensor, 0), my_tensor, 1)
    held, served = lax.optimization_barrier((held, served))
    held = doubled(held, my_tensor, 2)
    held, squares, served = lax.optimization_barrier((held, squares, served))
    kg_all = held.reshape(8 * rows, tokens)
    inverse_rms = 1.0 / jnp.sqrt(jnp.sum(squares, axis=0).reshape(tokens) / width + 1e-05)
    fresh_weight = served[0] + swap(served[0], "replica", PLANE)
    fresh_weight = [fresh_weight] + [swap(fresh_weight, "replica", bit) for bit in (1, 2, 3)]

    normed = (x * inverse_rms[:, None]).astype(SHORT)
    grad = lax.dot_general(kg_all, normed, (((1,), (0,)), ((), ())), preferred_element_type=WIDE).astype(SHORT)
    grad = grad.reshape(8, PLANE, part, cols).transpose(1, 0, 2, 3)
    grad = jnp.sum(exchange_x(grad).astype(WIDE), axis=0).astype(SHORT)
    grad_rows = lax.all_to_all(grad, "tensor", 0, 0, tiled=True)

    sent, restored_weight = assemble(failed_replica, own_weight, fresh_weight)
    sent, grad_rows = lax.optimization_barrier((sent, grad_rows))
    weight_cols = lax.all_to_all(sent, "tensor", 0, 0, tiled=True).reshape(8 * rows, cols)
    grad_rows = grad_rows.transpose(1, 0, 2).reshape(part, width)
    mean_rows = (grad_rows.astype(WIDE) + swap(grad_rows, "replica", PLANE).astype(WIDE)) / copies

    keys = lax.dot_general(weight_cols, normed, (((1,), (1,)), ((), ())), preferred_element_type=WIDE).astype(SHORT)
    feature = lax.dot_general(kg_all, weight_cols, (((0,), (0,)), ((), ())), preferred_element_type=WIDE)
    product = jnp.sum(feature * x, axis=1).reshape(-1, 128)
    for bit in (1, 2, 4):
        product = product + swap(product, "tensor", bit)
    product = product.reshape(tokens, 1)
    scale = inverse_rms[:, None]
    input_grad = scale * feature - scale * scale * scale * x * product / width
    outgoing = from_behind(input_grad.astype(SHORT), "section", -1)
    got = lax.all_to_all(keys.reshape(8, rows, tokens), "tensor", 0, 0, tiled=True)
    key_out = jnp.sum(got.astype(WIDE), axis=0).T.astype(SHORT)

    def checksum(source):
        shaped = source.reshape(-1, nchunk, 128)
        mixed = jnp.einsum("jnc,cp->jnp", shaped, probe_matrix, precision=lax.Precision.HIGHEST)
        return mixed.reshape(-1, nchunk * probe_matrix.shape[1])

    served_moments = served[1:].astype(WIDE)
    served_update = adam(served_moments[0], served_moments[1], mean_rows).astype(SHORT)
    served_sums = checksum(served_moments.reshape(2 * part, width)).astype(SHORT).reshape(2, width)
    mine = jnp.concatenate([served_update, served_sums], axis=0)
    other = swap(mine, "replica", PLANE)
    fresh_update = jnp.where(columns, mine[:part], other[:part])
    fresh_sums = mine[part:] + other[part:]
    shared = jnp.concatenate([mean_rows.astype(SHORT), fresh_update, fresh_sums], axis=0)
    shared = gather_x(tied(shared, weight_cols))
    mean_grad = shared[:, :part].reshape(rows, width).astype(WIDE)
    fresh_update = shared[:, part : 2 * part].reshape(rows, width).astype(WIDE)
    fresh_sums = shared[:, 2 * part :].reshape(PLANE, 2, part, -1).transpose(1, 0, 2, 3).reshape(2, rows, -1).astype(WIDE)
    update = jnp.where(is_failed, fresh_update, adam(own_first, own_second, mean_grad))
    own_sums = jnp.stack([checksum(own_first), checksum(own_second)])
    checksums = jnp.where(is_failed, fresh_sums, own_sums)
    weight_checksums = checksum(restored_weight.astype(WIDE))
    return (key_out[None, None], outgoing[None, None], update[None, None], checksums[None, None], weight_checksums[None, None])


def solution(mesh):
    by_rows = P("replica", "section", "tensor", None)
    by_features = P("replica", "section", None, "tensor")
    return jax.shard_map(
        shards,
        mesh=mesh,
        in_specs=(by_features, by_features, by_rows, by_rows, by_rows, P(), P(), P()),
        out_specs=(by_features, by_features, by_rows, P("replica", "section", None, "tensor", None), by_rows),
        check_vma=False,
    )
```

```python
import jax
import jax.numpy as jnp
from jax import lax
from jax.experimental import pallas as pl
from jax.experimental.pallas import tpu as pltpu
from jax.sharding import PartitionSpec as P

SHORT = jnp.bfloat16
WIDE = jnp.float32
PLANE = 4
SPAN = 128


def from_behind(block, axis, distance):
    n = lax.axis_size(axis)
    return lax.ppermute(block, axis, [((i - distance) % n, i) for i in range(n)])


def swap(block, axis, bit):
    return lax.ppermute(block, axis, [(i, i ^ bit) for i in range(lax.axis_size(axis))])


def exchange_x(block):
    groups = [[0, 1, 2, 3], [4, 5, 6, 7]]
    return lax.all_to_all(block, "replica", 0, 0, axis_index_groups=groups, tiled=True)


def two_halves(value):
    high = value.astype(SHORT)
    return high, (value - high.astype(WIDE)).astype(SHORT)


def in_order(held, mine, bits):
    for bit in bits:
        split = held.reshape((held.shape[0] // (2 * bit), 2, bit) + held.shape[1:])
        held = jnp.where((mine & bit) != 0, split[:, ::-1], split).reshape(held.shape)
    return held


def doubled(held, mine, axis):
    bit = 4 >> axis
    came = swap(held, "tensor", bit)
    high = (mine & bit) != 0
    return jnp.stack([jnp.where(high, came, held), jnp.where(high, held, came)], axis=axis)


def gather_x(block):
    held = jnp.stack([block] + [swap(block, "replica", bit) for bit in (1, 2, 3)])
    return in_order(held, lax.axis_index("replica") & 3, (2, 1))


def broadcast_x(block):
    return exchange_x(jnp.broadcast_to(block[None], (PLANE,) + block.shape))


def tied(value, *after):
    return lax.optimization_barrier((value,) + after)[0]


def serve_kernel(failed_ref, spans_ref, weight_ref, first_ref, second_ref, out_ref):
    section = lax.axis_index("section")
    me = lax.axis_index("replica")
    failed = failed_ref[section, lax.axis_index("tensor")]
    is_primary = (failed ^ PLANE) == me
    is_second = (failed ^ 1) == me
    part = out_ref.shape[2]
    for n in range(weight_ref.shape[1] // SPAN):
        listed = spans_ref[section, 0] == n
        for j in range(1, spans_ref.shape[1]):
            listed = listed | (spans_ref[section, j] == n)
        take = (listed & is_second) | (jnp.logical_not(listed) & is_primary)
        here = pl.ds(n * SPAN, SPAN)
        for k, ref in enumerate((weight_ref, first_ref, second_ref)):
            for x in range(PLANE):
                block = ref[x * part : (x + 1) * part, here].astype(SHORT)
                out_ref[x, k, :, here] = jnp.where(take, block, jnp.zeros_like(block))


def serve(failed, spans, weight, first, second):
    rows, width = weight.shape
    return pl.pallas_call(
        serve_kernel,
        out_shape=jax.ShapeDtypeStruct((PLANE, 3, rows // PLANE, width), SHORT),
        in_specs=[pl.BlockSpec(memory_space=pltpu.SMEM)] * 2 + [pl.BlockSpec(memory_space=pltpu.VMEM)] * 3,
        out_specs=pl.BlockSpec(memory_space=pltpu.VMEM),
        name="serve",
    )(failed, spans, weight, first, second)


def assemble_kernel(failed_ref, own_ref, fresh0_ref, fresh1_ref, fresh2_ref, fresh3_ref, grads_ref, sent_ref, restored_ref):
    me = lax.axis_index("replica")
    here = failed_ref[lax.axis_index("section"), lax.axis_index("tensor")] == me
    rows = own_ref.shape[0]
    groups, _, cols = sent_ref.shape
    part = fresh0_ref.shape[0]
    for k, fresh_ref in enumerate((fresh0_ref, fresh1_ref, fresh2_ref, fresh3_ref)):
        at = pl.ds(pl.multiple_of(((me & 3) ^ k) * part, part), part)
        for t in range(groups):
            span = pl.ds(t * cols, cols)
            block = jnp.where(here, fresh_ref[:, span], own_ref[at, span])
            restored_ref[at, span] = block
            sent_ref[t, at, :] = block
    for t in range(groups):
        total = grads_ref[0, t].astype(WIDE)
        for x in range(1, PLANE):
            total = total + grads_ref[x, t].astype(WIDE)
        sent_ref[t, rows:, :] = total.astype(SHORT)


def assemble(failed, own, fresh, grads):
    rows, width = own.shape
    _, groups, part, cols = grads.shape
    return pl.pallas_call(
        assemble_kernel,
        out_shape=(
            jax.ShapeDtypeStruct((groups, rows + part, cols), SHORT),
            jax.ShapeDtypeStruct((rows, width), SHORT),
        ),
        in_specs=[pl.BlockSpec(memory_space=pltpu.SMEM)] + [pl.BlockSpec(memory_space=pltpu.VMEM)] * 6,
        out_specs=(pl.BlockSpec(memory_space=pltpu.VMEM),) * 2,
        name="assemble",
    )(failed, own, *fresh, grads)


def adam(first, second, grad):
    one = 0.9 * first + 0.1 * grad
    two = 0.95 * second + 0.05 * (grad * grad)
    return one / (jnp.sqrt(two) + 1e-08)


def shards(activations, key_grads, weight, first_moment, second_moment, probe_matrix, failed_replica, resend_spans):
    copies = lax.axis_size("replica")
    my_replica = lax.axis_index("replica")
    my_section = lax.axis_index("section")
    my_tensor = lax.axis_index("tensor")
    failed = failed_replica[my_section, my_tensor]
    my_spans = resend_spans[my_section]
    own_weight = weight[0, 0]
    own_first = first_moment[0, 0]
    own_second = second_moment[0, 0]
    rows, width = own_weight.shape
    nchunk = width // 128
    listed = jnp.any(my_spans[:, None] == jnp.arange(nchunk, dtype=jnp.int32)[None, :], axis=0)
    columns = jnp.repeat(listed, 128)[None, :]
    primary = jnp.bitwise_xor(failed, PLANE)
    second = jnp.bitwise_xor(failed, 1)
    chosen = jnp.where(columns, my_replica == second, my_replica == primary)
    is_failed = my_replica == failed
    part = rows // PLANE

    local = activations[0, 0]
    tokens, cols = local.shape
    incoming = from_behind(local, "section", 1)
    x = incoming.astype(WIDE)

    mask = serve(failed_replica, resend_spans, own_weight, own_first, own_second)
    served = jnp.sum(exchange_x(mask).astype(WIDE), axis=0).astype(SHORT)

    squares = jnp.sum(x * x, axis=1).reshape(1, -1, 128)
    squares = lax.all_to_all(jnp.broadcast_to(squares, (8,) + squares.shape[1:]), "tensor", 0, 0, tiled=True)
    held = tied(key_grads[0, 0].T, mask)
    held = doubled(doubled(held, my_tensor, 0), my_tensor, 1)
    held, served = lax.optimization_barrier((held, served))
    held = doubled(held, my_tensor, 2)
    held, squares, served = lax.optimization_barrier((held, squares, served))
    fresh_weight = served[0] + swap(served[0], "replica", PLANE)
    fresh_moments = served[1:] + swap(served[1:], "replica", PLANE)
    kg_all = held.reshape(8 * rows, tokens)
    inverse_rms = 1.0 / jnp.sqrt(jnp.sum(squares, axis=0).reshape(tokens) / width + 1e-05)
    fresh_weight = [fresh_weight] + [swap(fresh_weight, "replica", bit) for bit in (1, 2, 3)]

    normed = (x * inverse_rms[:, None]).astype(SHORT)
    grad = lax.dot_general(kg_all, normed, (((1,), (0,)), ((), ())), preferred_element_type=WIDE).astype(SHORT)
    grad = grad.reshape(8, PLANE, part, cols).transpose(1, 0, 2, 3)
    grad, fresh_moments = lax.optimization_barrier((exchange_x(grad), fresh_moments))

    sent, restored_weight = assemble(failed_replica, own_weight, fresh_weight, grad)
    own_first, own_second, restored_weight = lax.optimization_barrier((own_first, own_second, restored_weight))
    got = lax.all_to_all(sent, "tensor", 0, 0, tiled=True)
    weight_cols = got[:, :rows].reshape(8 * rows, cols)
    grad_rows = got[:, rows:].transpose(1, 0, 2).reshape(part, width)
    mean_rows = (grad_rows.astype(WIDE) + swap(grad_rows, "replica", PLANE).astype(WIDE)) / copies

    keys = lax.dot_general(weight_cols, normed, (((1,), (1,)), ((), ())), preferred_element_type=WIDE).astype(SHORT)
    feature = lax.dot_general(kg_all, weight_cols, (((0,), (0,)), ((), ())), preferred_element_type=WIDE)
    product = jnp.sum(feature * x, axis=1).reshape(-1, 128)
    for bit in (1, 2, 4):
        product = product + swap(product, "tensor", bit)
    product = product.reshape(tokens, 1)
    scale = inverse_rms[:, None]
    input_grad = scale * feature - scale * scale * scale * x * product / width
    outgoing = from_behind(input_grad.astype(SHORT), "section", -1)
    got = lax.all_to_all(keys.reshape(8, rows, tokens), "tensor", 0, 0, tiled=True)
    key_out = jnp.sum(got.astype(WIDE), axis=0).T.astype(SHORT)

    def checksum(source):
        shaped = source.reshape(-1, nchunk, 128)
        mixed = jnp.einsum("jnc,cp->jnp", shaped, probe_matrix, precision=lax.Precision.HIGHEST)
        return mixed.reshape(-1, nchunk * probe_matrix.shape[1])

    fresh = fresh_moments.astype(WIDE)
    fresh_update = adam(fresh[0], fresh[1], mean_rows).astype(SHORT)
    fresh_sums = checksum(fresh.reshape(2 * part, width)).astype(SHORT).reshape(2, width)
    shared = gather_x(jnp.concatenate([mean_rows.astype(SHORT), fresh_update, fresh_sums], axis=0))
    mean_grad = shared[:, :part].reshape(rows, width).astype(WIDE)
    fresh_update = shared[:, part : 2 * part].reshape(rows, width).astype(WIDE)
    fresh_sums = shared[:, 2 * part :].reshape(PLANE, 2, part, -1).transpose(1, 0, 2, 3).reshape(2, rows, -1).astype(WIDE)
    update = jnp.where(is_failed, fresh_update, adam(own_first, own_second, mean_grad))
    own_sums = jnp.stack([checksum(own_first), checksum(own_second)])
    checksums = jnp.where(is_failed, fresh_sums, own_sums)
    weight_checksums = checksum(restored_weight.astype(WIDE))
    return (key_out[None, None], outgoing[None, None], update[None, None], checksums[None, None], weight_checksums[None, None])


def solution(mesh):
    by_rows = P("replica", "section", "tensor", None)
    by_features = P("replica", "section", None, "tensor")
    return jax.shard_map(
        shards,
        mesh=mesh,
        in_specs=(by_features, by_features, by_rows, by_rows, by_rows, P(), P(), P()),
        out_specs=(by_features, by_features, by_rows, P("replica", "section", None, "tensor", None), by_rows),
        check_vma=False,
    )
```

```python
import jax
import jax.numpy as jnp
from jax import lax
from jax.experimental import pallas as pl
from jax.experimental.pallas import tpu as pltpu
from jax.sharding import PartitionSpec as P

SHORT = jnp.bfloat16
WIDE = jnp.float32
PLANE = 4
SPAN = 128


def from_behind(block, axis, distance):
    n = lax.axis_size(axis)
    return lax.ppermute(block, axis, [((i - distance) % n, i) for i in range(n)])


def swap(block, axis, bit):
    return lax.ppermute(block, axis, [(i, i ^ bit) for i in range(lax.axis_size(axis))])


def exchange_x(block):
    groups = [[0, 1, 2, 3], [4, 5, 6, 7]]
    return lax.all_to_all(block, "replica", 0, 0, axis_index_groups=groups, tiled=True)


def two_halves(value):
    high = value.astype(SHORT)
    return high, (value - high.astype(WIDE)).astype(SHORT)


def in_order(held, mine, bits):
    for bit in bits:
        split = held.reshape((held.shape[0] // (2 * bit), 2, bit) + held.shape[1:])
        held = jnp.where((mine & bit) != 0, split[:, ::-1], split).reshape(held.shape)
    return held


def doubled(held, mine, axis):
    bit = 4 >> axis
    came = swap(held, "tensor", bit)
    high = (mine & bit) != 0
    return jnp.stack([jnp.where(high, came, held), jnp.where(high, held, came)], axis=axis)


def gather_x(block):
    held = jnp.stack([block] + [swap(block, "replica", bit) for bit in (1, 2, 3)])
    return in_order(held, lax.axis_index("replica") & 3, (2, 1))


def broadcast_x(block):
    return exchange_x(jnp.broadcast_to(block[None], (PLANE,) + block.shape))


def tied(value, *after):
    return lax.optimization_barrier((value,) + after)[0]


def places(spans_ref, section, count):
    ahead = [jnp.int32(0), jnp.int32(count - spans_ref.shape[1])]
    found = []
    for n in range(count):
        listed = spans_ref[section, 0] == n
        for j in range(1, spans_ref.shape[1]):
            listed = listed | (spans_ref[section, j] == n)
        bit = listed.astype(jnp.int32)
        slot = jnp.where(listed, ahead[1], ahead[0])
        found.append((listed, pl.ds(pl.multiple_of(slot * SPAN, SPAN), SPAN)))
        ahead = [ahead[0] + 1 - bit, ahead[1] + bit]
    return found


def serve_kernel(failed_ref, spans_ref, weight_ref, first_ref, second_ref, out_ref):
    section = lax.axis_index("section")
    me = lax.axis_index("replica")
    failed = failed_ref[section, lax.axis_index("tensor")]
    is_primary = (failed ^ PLANE) == me
    is_second = (failed ^ 1) == me
    part = out_ref.shape[2]
    for n, (listed, place) in enumerate(places(spans_ref, section, weight_ref.shape[1] // SPAN)):
        take = (listed & is_second) | (jnp.logical_not(listed) & is_primary)
        for k, ref in enumerate((weight_ref, first_ref, second_ref)):
            for x in range(PLANE):
                block = ref[x * part : (x + 1) * part, n * SPAN : (n + 1) * SPAN].astype(SHORT)
                out_ref[x, k, :, place] = jnp.where(take, block, jnp.zeros_like(block))


def serve(failed, spans, weight, first, second):
    rows, width = weight.shape
    return pl.pallas_call(
        serve_kernel,
        out_shape=jax.ShapeDtypeStruct((PLANE, 3, rows // PLANE, width), SHORT),
        in_specs=[pl.BlockSpec(memory_space=pltpu.SMEM)] * 2 + [pl.BlockSpec(memory_space=pltpu.VMEM)] * 3,
        out_specs=pl.BlockSpec(memory_space=pltpu.VMEM),
        name="serve",
    )(failed, spans, weight, first, second)


def unpack_kernel(spans_ref, placed_ref, out_ref):
    section = lax.axis_index("section")
    for n, (_, place) in enumerate(places(spans_ref, section, out_ref.shape[2] // SPAN)):
        for k in range(out_ref.shape[0]):
            out_ref[k, :, n * SPAN : (n + 1) * SPAN] = placed_ref[k, :, place]


def unpack(spans, placed):
    return pl.pallas_call(
        unpack_kernel,
        out_shape=jax.ShapeDtypeStruct(placed.shape, placed.dtype),
        in_specs=[pl.BlockSpec(memory_space=pltpu.SMEM), pl.BlockSpec(memory_space=pltpu.VMEM)],
        out_specs=pl.BlockSpec(memory_space=pltpu.VMEM),
        name="unpack",
    )(spans, placed)


def assemble_kernel(failed_ref, spans_ref, own_ref, fresh0_ref, fresh1_ref, fresh2_ref, fresh3_ref, grads_ref, sent_ref, restored_ref):
    section = lax.axis_index("section")
    me = lax.axis_index("replica")
    here = failed_ref[section, lax.axis_index("tensor")] == me
    rows, width = own_ref.shape
    groups, _, cols = sent_ref.shape
    part = fresh0_ref.shape[0]
    apart = cols // SPAN
    spans = places(spans_ref, section, width // SPAN)
    for k, fresh_ref in enumerate((fresh0_ref, fresh1_ref, fresh2_ref, fresh3_ref)):
        at = pl.ds(pl.multiple_of(((me & 3) ^ k) * part, part), part)
        for n, (_, place) in enumerate(spans):
            block = jnp.where(here, fresh_ref[:, place], own_ref[at, n * SPAN : (n + 1) * SPAN])
            restored_ref[at, n * SPAN : (n + 1) * SPAN] = block
            sent_ref[n // apart, at, (n % apart) * SPAN : (n % apart + 1) * SPAN] = block
    for t in range(groups):
        total = grads_ref[0, t].astype(WIDE)
        for x in range(1, PLANE):
            total = total + grads_ref[x, t].astype(WIDE)
        sent_ref[t, rows:, :] = total.astype(SHORT)


def assemble(failed, spans, own, fresh, grads):
    rows, width = own.shape
    _, groups, part, cols = grads.shape
    return pl.pallas_call(
        assemble_kernel,
        out_shape=(
            jax.ShapeDtypeStruct((groups, rows + part, cols), SHORT),
            jax.ShapeDtypeStruct((rows, width), SHORT),
        ),
        in_specs=[pl.BlockSpec(memory_space=pltpu.SMEM)] * 2 + [pl.BlockSpec(memory_space=pltpu.VMEM)] * 6,
        out_specs=(pl.BlockSpec(memory_space=pltpu.VMEM),) * 2,
        name="assemble",
    )(failed, spans, own, *fresh, grads)


def adam(first, second, grad):
    one = 0.9 * first + 0.1 * grad
    two = 0.95 * second + 0.05 * (grad * grad)
    return one / (jnp.sqrt(two) + 1e-08)


def shards(activations, key_grads, weight, first_moment, second_moment, probe_matrix, failed_replica, resend_spans):
    copies = lax.axis_size("replica")
    my_replica = lax.axis_index("replica")
    my_section = lax.axis_index("section")
    my_tensor = lax.axis_index("tensor")
    failed = failed_replica[my_section, my_tensor]
    my_spans = resend_spans[my_section]
    own_weight = weight[0, 0]
    own_first = first_moment[0, 0]
    own_second = second_moment[0, 0]
    rows, width = own_weight.shape
    nchunk = width // 128
    is_failed = my_replica == failed
    part = rows // PLANE

    local = activations[0, 0]
    tokens, cols = local.shape
    squares = jnp.sum(jnp.square(local.astype(WIDE)), axis=1).reshape(-1, 128)
    squares = from_behind(squares, "section", 1).reshape(1, tokens)
    incoming = from_behind(local, "section", 1)
    x = incoming.astype(WIDE)

    mask = serve(failed_replica, resend_spans, own_weight, own_first, own_second)
    served = jnp.sum(exchange_x(mask).astype(WIDE), axis=0).astype(SHORT)

    high, low = two_halves(squares)
    extra = jnp.concatenate([high, low, jnp.zeros((6, tokens), SHORT)], axis=0)
    held = jnp.concatenate([tied(key_grads[0, 0].T, mask), extra], axis=0)
    held = doubled(doubled(held, my_tensor, 0), my_tensor, 1)
    held, served = lax.optimization_barrier((held, served))
    cross = width - my_spans.shape[0] * SPAN
    crossed = served[:, :, :cross] + swap(served[:, :, :cross], "replica", PLANE)
    fresh = jnp.concatenate([crossed, served[:, :, cross:]], axis=2)
    fresh_weight = [fresh[0]] + [swap(fresh[0], "replica", bit) for bit in (1, 2, 3)]
    held = doubled(held, my_tensor, 2).reshape(8, -1, tokens)
    kg_all = held[:, :rows].reshape(8 * rows, tokens)
    squares = jnp.sum(held[:, rows].astype(WIDE) + held[:, rows + 1].astype(WIDE), axis=0)
    inverse_rms = 1.0 / jnp.sqrt(squares / width + 1e-05)

    normed = (x * inverse_rms[:, None]).astype(SHORT)
    grad = lax.dot_general(kg_all, normed, (((1,), (0,)), ((), ())), preferred_element_type=WIDE).astype(SHORT)
    grad = grad.reshape(8, PLANE, part, cols).transpose(1, 0, 2, 3)
    grad = exchange_x(grad)

    sent, restored_weight = assemble(failed_replica, resend_spans, own_weight, fresh_weight, grad)
    own_first, own_second, restored_weight, fresh = lax.optimization_barrier((own_first, own_second, restored_weight, fresh))
    got = lax.all_to_all(sent, "tensor", 0, 0, tiled=True)
    weight_cols = got[:, :rows].reshape(8 * rows, cols)
    grad_rows = got[:, rows:].transpose(1, 0, 2).reshape(part, width)
    mean_rows = (grad_rows.astype(WIDE) + swap(grad_rows, "replica", PLANE).astype(WIDE)) / copies

    keys = lax.dot_general(weight_cols, normed, (((1,), (1,)), ((), ())), preferred_element_type=WIDE).astype(SHORT)
    feature = lax.dot_general(kg_all, weight_cols, (((0,), (0,)), ((), ())), preferred_element_type=WIDE)
    product = jnp.sum(feature * x, axis=1).reshape(-1, 128)
    for bit in (1, 2, 4):
        product = product + swap(product, "tensor", bit)
    product = product.reshape(tokens, 1)
    scale = inverse_rms[:, None]
    input_grad = scale * feature - scale * scale * scale * x * product / width
    outgoing = from_behind(input_grad.astype(SHORT), "section", -1)
    got = lax.all_to_all(keys.reshape(8, rows, tokens), "tensor", 0, 0, tiled=True)
    key_out = jnp.sum(got.astype(WIDE), axis=0).T.astype(SHORT)

    def checksum(source):
        shaped = source.reshape(-1, nchunk, 128)
        mixed = jnp.einsum("jnc,cp->jnp", shaped, probe_matrix, precision=lax.Precision.HIGHEST)
        return mixed.reshape(-1, nchunk * probe_matrix.shape[1])

    fresh = unpack(resend_spans, fresh[1:]).astype(WIDE)
    fresh_update = adam(fresh[0], fresh[1], mean_rows).astype(SHORT)
    fresh_sums = checksum(fresh.reshape(2 * part, width)).astype(SHORT).reshape(2, width)
    shared = gather_x(jnp.concatenate([mean_rows.astype(SHORT), fresh_update, fresh_sums], axis=0))
    mean_grad = shared[:, :part].reshape(rows, width).astype(WIDE)
    fresh_update = shared[:, part : 2 * part].reshape(rows, width).astype(WIDE)
    fresh_sums = shared[:, 2 * part :].reshape(PLANE, 2, part, -1).transpose(1, 0, 2, 3).reshape(2, rows, -1).astype(WIDE)
    update = jnp.where(is_failed, fresh_update, adam(own_first, own_second, mean_grad))
    own_sums = jnp.stack([checksum(own_first), checksum(own_second)])
    checksums = jnp.where(is_failed, fresh_sums, own_sums)
    weight_checksums = checksum(restored_weight.astype(WIDE))
    return (key_out[None, None], outgoing[None, None], update[None, None], checksums[None, None], weight_checksums[None, None])


def solution(mesh):
    by_rows = P("replica", "section", "tensor", None)
    by_features = P("replica", "section", None, "tensor")
    return jax.shard_map(
        shards,
        mesh=mesh,
        in_specs=(by_features, by_features, by_rows, by_rows, by_rows, P(), P(), P()),
        out_specs=(by_features, by_features, by_rows, P("replica", "section", None, "tensor", None), by_rows),
        check_vma=False,
    )
```

```python
import jax
import jax.numpy as jnp
from jax import lax
from jax.experimental import pallas as pl
from jax.experimental.pallas import tpu as pltpu
from jax.sharding import PartitionSpec as P

SHORT = jnp.bfloat16
WIDE = jnp.float32
PLANE = 4
SPAN = 128


def from_behind(block, axis, distance):
    n = lax.axis_size(axis)
    return lax.ppermute(block, axis, [((i - distance) % n, i) for i in range(n)])


def swap(block, axis, bit):
    return lax.ppermute(block, axis, [(i, i ^ bit) for i in range(lax.axis_size(axis))])


def exchange_x(block):
    groups = [[0, 1, 2, 3], [4, 5, 6, 7]]
    return lax.all_to_all(block, "replica", 0, 0, axis_index_groups=groups, tiled=True)


def two_halves(value):
    high = value.astype(SHORT)
    return high, (value - high.astype(WIDE)).astype(SHORT)


def in_order(held, mine, bits):
    for bit in bits:
        split = held.reshape((held.shape[0] // (2 * bit), 2, bit) + held.shape[1:])
        held = jnp.where((mine & bit) != 0, split[:, ::-1], split).reshape(held.shape)
    return held


def doubled(held, mine, axis, part=None):
    bit = 4 >> axis
    sent = held
    if part is not None:
        high, low = two_halves(part)
        rows = held.reshape(-1, held.shape[-1])
        sent = jnp.concatenate([rows, high, low, jnp.zeros((6, held.shape[-1]), SHORT)], axis=0)
    came = swap(sent, "tensor", bit)
    if part is not None:
        part = part + came[-8:-7].astype(WIDE) + came[-7:-6].astype(WIDE)
        came = came[:-8].reshape(held.shape)
    upper = (mine & bit) != 0
    held = jnp.stack([jnp.where(upper, came, held), jnp.where(upper, held, came)], axis=axis)
    return held if part is None else (held, part)


def gather_x(block):
    held = jnp.stack([block] + [swap(block, "replica", bit) for bit in (1, 2, 3)])
    return in_order(held, lax.axis_index("replica") & 3, (2, 1))


def broadcast_x(block):
    return exchange_x(jnp.broadcast_to(block[None], (PLANE,) + block.shape))


def tied(value, *after):
    return lax.optimization_barrier((value,) + after)[0]


def places(spans_ref, section, count):
    ahead = [jnp.int32(0), jnp.int32(count - spans_ref.shape[1])]
    found = []
    for n in range(count):
        listed = spans_ref[section, 0] == n
        for j in range(1, spans_ref.shape[1]):
            listed = listed | (spans_ref[section, j] == n)
        bit = listed.astype(jnp.int32)
        slot = jnp.where(listed, ahead[1], ahead[0])
        found.append((listed, pl.ds(pl.multiple_of(slot * SPAN, SPAN), SPAN)))
        ahead = [ahead[0] + 1 - bit, ahead[1] + bit]
    return found


def serve_kernel(failed_ref, spans_ref, weight_ref, first_ref, second_ref, weight_out_ref, moments_out_ref):
    section = lax.axis_index("section")
    me = lax.axis_index("replica")
    failed = failed_ref[section, lax.axis_index("tensor")]
    is_primary = (failed ^ PLANE) == me
    is_second = (failed ^ 1) == me
    part = weight_out_ref.shape[1]
    for n, (listed, place) in enumerate(places(spans_ref, section, weight_ref.shape[1] // SPAN)):
        take = (listed & is_second) | (jnp.logical_not(listed) & is_primary)
        here = pl.ds(n * SPAN, SPAN)
        for x in range(PLANE):
            at = pl.ds(x * part, part)
            block = weight_ref[at, here]
            weight_out_ref[x, :, place] = jnp.where(take, block, jnp.zeros_like(block))
            for k, ref in enumerate((first_ref, second_ref)):
                block = ref[at, here].astype(SHORT)
                moments_out_ref[x, k, :, place] = jnp.where(take, block, jnp.zeros_like(block))


def serve(failed, spans, weight, first, second):
    rows, width = weight.shape
    return pl.pallas_call(
        serve_kernel,
        out_shape=(
            jax.ShapeDtypeStruct((PLANE, rows // PLANE, width), SHORT),
            jax.ShapeDtypeStruct((PLANE, 2, rows // PLANE, width), SHORT),
        ),
        in_specs=[pl.BlockSpec(memory_space=pltpu.SMEM)] * 2 + [pl.BlockSpec(memory_space=pltpu.VMEM)] * 3,
        out_specs=(pl.BlockSpec(memory_space=pltpu.VMEM),) * 2,
        name="serve",
    )(failed, spans, weight, first, second)


def unpack_kernel(spans_ref, placed_ref, out_ref):
    section = lax.axis_index("section")
    for n, (_, place) in enumerate(places(spans_ref, section, out_ref.shape[2] // SPAN)):
        for k in range(out_ref.shape[0]):
            out_ref[k, :, n * SPAN : (n + 1) * SPAN] = placed_ref[k, :, place]


def unpack(spans, placed):
    return pl.pallas_call(
        unpack_kernel,
        out_shape=jax.ShapeDtypeStruct(placed.shape, placed.dtype),
        in_specs=[pl.BlockSpec(memory_space=pltpu.SMEM), pl.BlockSpec(memory_space=pltpu.VMEM)],
        out_specs=pl.BlockSpec(memory_space=pltpu.VMEM),
        name="unpack",
    )(spans, placed)


def assemble_kernel(failed_ref, spans_ref, own_ref, fresh0_ref, fresh1_ref, fresh2_ref, fresh3_ref, grads_ref, sent_ref, restored_ref):
    section = lax.axis_index("section")
    me = lax.axis_index("replica")
    here = failed_ref[section, lax.axis_index("tensor")] == me
    rows, width = own_ref.shape
    groups, _, cols = sent_ref.shape
    part = fresh0_ref.shape[0]
    apart = cols // SPAN
    spans = places(spans_ref, section, width // SPAN)
    for k, fresh_ref in enumerate((fresh0_ref, fresh1_ref, fresh2_ref, fresh3_ref)):
        at = pl.ds(pl.multiple_of(((me & 3) ^ k) * part, part), part)
        for n, (_, place) in enumerate(spans):
            block = jnp.where(here, fresh_ref[:, place], own_ref[at, n * SPAN : (n + 1) * SPAN])
            restored_ref[at, n * SPAN : (n + 1) * SPAN] = block
            sent_ref[n // apart, at, (n % apart) * SPAN : (n % apart + 1) * SPAN] = block
    for t in range(groups):
        total = grads_ref[0, t].astype(WIDE)
        for x in range(1, PLANE):
            total = total + grads_ref[x, t].astype(WIDE)
        sent_ref[t, rows:, :] = total.astype(SHORT)


def assemble(failed, spans, own, fresh, grads):
    rows, width = own.shape
    _, groups, part, cols = grads.shape
    return pl.pallas_call(
        assemble_kernel,
        out_shape=(
            jax.ShapeDtypeStruct((groups, rows + part, cols), SHORT),
            jax.ShapeDtypeStruct((rows, width), SHORT),
        ),
        in_specs=[pl.BlockSpec(memory_space=pltpu.SMEM)] * 2 + [pl.BlockSpec(memory_space=pltpu.VMEM)] * 6,
        out_specs=(pl.BlockSpec(memory_space=pltpu.VMEM),) * 2,
        name="assemble",
    )(failed, spans, own, *fresh, grads)


def adam(first, second, grad):
    one = 0.9 * first + 0.1 * grad
    two = 0.95 * second + 0.05 * (grad * grad)
    return one / (jnp.sqrt(two) + 1e-08)


def shards(activations, key_grads, weight, first_moment, second_moment, probe_matrix, failed_replica, resend_spans):
    copies = lax.axis_size("replica")
    my_replica = lax.axis_index("replica")
    my_section = lax.axis_index("section")
    my_tensor = lax.axis_index("tensor")
    failed = failed_replica[my_section, my_tensor]
    my_spans = resend_spans[my_section]
    own_weight = weight[0, 0]
    own_first = first_moment[0, 0]
    own_second = second_moment[0, 0]
    rows, width = own_weight.shape
    nchunk = width // 128
    is_failed = my_replica == failed
    part = rows // PLANE

    local = activations[0, 0]
    tokens, cols = local.shape
    squares = jnp.sum(jnp.square(local.astype(WIDE)), axis=1).reshape(-1, 128)
    squares = from_behind(squares, "section", 1).reshape(1, tokens)
    incoming = from_behind(local, "section", 1)
    x = incoming.astype(WIDE)

    def summed(parts):
        return jnp.sum(parts.astype(WIDE), axis=0).astype(SHORT)

    cross = width - my_spans.shape[0] * SPAN

    def both_planes(served):
        crossed = served[..., :cross] + swap(served[..., :cross], "replica", PLANE)
        return jnp.concatenate([crossed, served[..., cross:]], axis=-1)

    mask_weight, mask_moments = serve(failed_replica, resend_spans, own_weight, own_first, own_second)
    served_weight = summed(exchange_x(mask_weight))

    held = doubled(tied(key_grads[0, 0].T, mask_weight), my_tensor, 0)
    squares = squares + swap(squares, "tensor", 4)
    held, served_weight, mask_moments, squares = lax.optimization_barrier((held, served_weight, mask_moments, squares))
    held, squares = doubled(held, my_tensor, 1, squares)
    held, served_weight, mask_moments = lax.optimization_barrier((held, served_weight, mask_moments))
    served_moments = summed(exchange_x(mask_moments))
    fresh_weight = both_planes(served_weight)
    fresh_weight = [fresh_weight] + [swap(fresh_weight, "replica", bit) for bit in (1, 2, 3)]
    held, squares = doubled(held, my_tensor, 2, squares)
    kg_all = held.reshape(8 * rows, tokens)
    inverse_rms = 1.0 / jnp.sqrt(squares.reshape(tokens) / width + 1e-05)

    normed = (x * inverse_rms[:, None]).astype(SHORT)
    grad = lax.dot_general(kg_all, normed, (((1,), (0,)), ((), ())), preferred_element_type=WIDE).astype(SHORT)
    grad = grad.reshape(8, PLANE, part, cols).transpose(1, 0, 2, 3)
    grad, served_moments = lax.optimization_barrier((grad, served_moments))
    grad = exchange_x(grad)
    fresh = both_planes(served_moments)

    sent, restored_weight = assemble(failed_replica, resend_spans, own_weight, fresh_weight, grad)
    own_first, own_second, restored_weight, fresh = lax.optimization_barrier((own_first, own_second, restored_weight, fresh))
    got = lax.all_to_all(sent, "tensor", 0, 0, tiled=True)
    weight_cols = got[:, :rows].reshape(8 * rows, cols)
    grad_rows = got[:, rows:].transpose(1, 0, 2).reshape(part, width)
    mean_rows = (grad_rows.astype(WIDE) + swap(grad_rows, "replica", PLANE).astype(WIDE)) / copies

    keys = lax.dot_general(weight_cols, normed, (((1,), (1,)), ((), ())), preferred_element_type=WIDE).astype(SHORT)
    feature = lax.dot_general(kg_all, weight_cols, (((0,), (0,)), ((), ())), preferred_element_type=WIDE)
    product = jnp.sum(feature * x, axis=1).reshape(-1, 128)
    for bit in (1, 2, 4):
        product = product + swap(product, "tensor", bit)
    product = product.reshape(tokens, 1)
    scale = inverse_rms[:, None]
    input_grad = scale * feature - scale * scale * scale * x * product / width
    outgoing = from_behind(input_grad.astype(SHORT), "section", -1)
    got = lax.all_to_all(keys.reshape(8, rows, tokens), "tensor", 0, 0, tiled=True)
    key_out = jnp.sum(got.astype(WIDE), axis=0).T.astype(SHORT)

    def checksum(source):
        shaped = source.reshape(-1, nchunk, 128)
        mixed = jnp.einsum("jnc,cp->jnp", shaped, probe_matrix, precision=lax.Precision.HIGHEST)
        return mixed.reshape(-1, nchunk * probe_matrix.shape[1])

    fresh = unpack(resend_spans, fresh).astype(WIDE)
    fresh_update = adam(fresh[0], fresh[1], mean_rows).astype(SHORT)
    fresh_sums = checksum(fresh.reshape(2 * part, width)).astype(SHORT).reshape(2, width)
    shared = gather_x(jnp.concatenate([mean_rows.astype(SHORT), fresh_update, fresh_sums], axis=0))
    mean_grad = shared[:, :part].reshape(rows, width).astype(WIDE)
    fresh_update = shared[:, part : 2 * part].reshape(rows, width).astype(WIDE)
    fresh_sums = shared[:, 2 * part :].reshape(PLANE, 2, part, -1).transpose(1, 0, 2, 3).reshape(2, rows, -1).astype(WIDE)
    update = jnp.where(is_failed, fresh_update, adam(own_first, own_second, mean_grad))
    own_sums = jnp.stack([checksum(own_first), checksum(own_second)])
    checksums = jnp.where(is_failed, fresh_sums, own_sums)
    weight_checksums = checksum(restored_weight.astype(WIDE))
    return (key_out[None, None], outgoing[None, None], update[None, None], checksums[None, None], weight_checksums[None, None])


def solution(mesh):
    by_rows = P("replica", "section", "tensor", None)
    by_features = P("replica", "section", None, "tensor")
    return jax.shard_map(
        shards,
        mesh=mesh,
        in_specs=(by_features, by_features, by_rows, by_rows, by_rows, P(), P(), P()),
        out_specs=(by_features, by_features, by_rows, P("replica", "section", None, "tensor", None), by_rows),
        check_vma=False,
    )
```

```python
import jax
import jax.numpy as jnp
from jax import lax
from jax.experimental import pallas as pl
from jax.experimental.pallas import tpu as pltpu
from jax.sharding import PartitionSpec as P

SHORT = jnp.bfloat16
WIDE = jnp.float32
PLANE = 4
SPAN = 128


def from_behind(block, axis, distance):
    n = lax.axis_size(axis)
    return lax.ppermute(block, axis, [((i - distance) % n, i) for i in range(n)])


def swap(block, axis, bit):
    return lax.ppermute(block, axis, [(i, i ^ bit) for i in range(lax.axis_size(axis))])


def exchange_x(block):
    groups = [[0, 1, 2, 3], [4, 5, 6, 7]]
    return lax.all_to_all(block, "replica", 0, 0, axis_index_groups=groups, tiled=True)


def two_halves(value):
    high = value.astype(SHORT)
    return high, (value - high.astype(WIDE)).astype(SHORT)


def in_order(held, mine, bits):
    for bit in bits:
        split = held.reshape((held.shape[0] // (2 * bit), 2, bit) + held.shape[1:])
        held = jnp.where((mine & bit) != 0, split[:, ::-1], split).reshape(held.shape)
    return held


def doubled(held, mine, axis):
    bit = 4 >> axis
    came = swap(held, "tensor", bit)
    high = (mine & bit) != 0
    return jnp.stack([jnp.where(high, came, held), jnp.where(high, held, came)], axis=axis)


def gather_x(block):
    held = jnp.stack([block] + [swap(block, "replica", bit) for bit in (1, 2, 3)])
    return in_order(held, lax.axis_index("replica") & 3, (2, 1))


def broadcast_x(block):
    return exchange_x(jnp.broadcast_to(block[None], (PLANE,) + block.shape))


def tied(value, *after):
    return lax.optimization_barrier((value,) + after)[0]


def places(spans_ref, section, count):
    ahead = [jnp.int32(0), jnp.int32(count - spans_ref.shape[1])]
    found = []
    for n in range(count):
        listed = spans_ref[section, 0] == n
        for j in range(1, spans_ref.shape[1]):
            listed = listed | (spans_ref[section, j] == n)
        bit = listed.astype(jnp.int32)
        slot = jnp.where(listed, ahead[1], ahead[0])
        found.append((listed, pl.ds(pl.multiple_of(slot * SPAN, SPAN), SPAN)))
        ahead = [ahead[0] + 1 - bit, ahead[1] + bit]
    return found


def serve_kernel(failed_ref, spans_ref, weight_ref, first_ref, second_ref, out_ref):
    section = lax.axis_index("section")
    me = lax.axis_index("replica")
    failed = failed_ref[section, lax.axis_index("tensor")]
    is_primary = (failed ^ PLANE) == me
    is_second = (failed ^ 1) == me
    part = out_ref.shape[2]
    for n, (listed, place) in enumerate(places(spans_ref, section, weight_ref.shape[1] // SPAN)):
        take = (listed & is_second) | (jnp.logical_not(listed) & is_primary)
        for k, ref in enumerate((weight_ref, first_ref, second_ref)):
            for x in range(PLANE):
                block = ref[x * part : (x + 1) * part, n * SPAN : (n + 1) * SPAN].astype(SHORT)
                out_ref[x, k, :, place] = jnp.where(take, block, jnp.zeros_like(block))


def serve(failed, spans, weight, first, second):
    rows, width = weight.shape
    return pl.pallas_call(
        serve_kernel,
        out_shape=jax.ShapeDtypeStruct((PLANE, 3, rows // PLANE, width), SHORT),
        in_specs=[pl.BlockSpec(memory_space=pltpu.SMEM)] * 2 + [pl.BlockSpec(memory_space=pltpu.VMEM)] * 3,
        out_specs=pl.BlockSpec(memory_space=pltpu.VMEM),
        name="serve",
    )(failed, spans, weight, first, second)


def unpack_kernel(spans_ref, placed_ref, out_ref):
    section = lax.axis_index("section")
    for n, (_, place) in enumerate(places(spans_ref, section, out_ref.shape[2] // SPAN)):
        for k in range(out_ref.shape[0]):
            out_ref[k, :, n * SPAN : (n + 1) * SPAN] = placed_ref[k, :, place]


def unpack(spans, placed):
    return pl.pallas_call(
        unpack_kernel,
        out_shape=jax.ShapeDtypeStruct(placed.shape, placed.dtype),
        in_specs=[pl.BlockSpec(memory_space=pltpu.SMEM), pl.BlockSpec(memory_space=pltpu.VMEM)],
        out_specs=pl.BlockSpec(memory_space=pltpu.VMEM),
        name="unpack",
    )(spans, placed)


def assemble_kernel(failed_ref, spans_ref, own_ref, fresh0_ref, fresh1_ref, fresh2_ref, fresh3_ref, grads_ref, sent_ref, restored_ref):
    section = lax.axis_index("section")
    me = lax.axis_index("replica")
    here = failed_ref[section, lax.axis_index("tensor")] == me
    rows, width = own_ref.shape
    groups, _, cols = sent_ref.shape
    part = fresh0_ref.shape[0]
    apart = cols // SPAN
    spans = places(spans_ref, section, width // SPAN)
    for k, fresh_ref in enumerate((fresh0_ref, fresh1_ref, fresh2_ref, fresh3_ref)):
        at = pl.ds(pl.multiple_of(((me & 3) ^ k) * part, part), part)
        for n, (_, place) in enumerate(spans):
            block = jnp.where(here, fresh_ref[:, place], own_ref[at, n * SPAN : (n + 1) * SPAN])
            restored_ref[at, n * SPAN : (n + 1) * SPAN] = block
            sent_ref[n // apart, at, (n % apart) * SPAN : (n % apart + 1) * SPAN] = block
    for t in range(groups):
        sent_ref[t, rows:, :] = grads_ref[t]


def assemble(failed, spans, own, fresh, grads):
    rows, width = own.shape
    groups, part, cols = grads.shape
    return pl.pallas_call(
        assemble_kernel,
        out_shape=(
            jax.ShapeDtypeStruct((groups, rows + part, cols), SHORT),
            jax.ShapeDtypeStruct((rows, width), SHORT),
        ),
        in_specs=[pl.BlockSpec(memory_space=pltpu.SMEM)] * 2 + [pl.BlockSpec(memory_space=pltpu.VMEM)] * 6,
        out_specs=(pl.BlockSpec(memory_space=pltpu.VMEM),) * 2,
        name="assemble",
    )(failed, spans, own, *fresh, grads)


def adam(first, second, grad):
    one = 0.9 * first + 0.1 * grad
    two = 0.95 * second + 0.05 * (grad * grad)
    return one / (jnp.sqrt(two) + 1e-08)


def shards(activations, key_grads, weight, first_moment, second_moment, probe_matrix, failed_replica, resend_spans):
    copies = lax.axis_size("replica")
    my_replica = lax.axis_index("replica")
    my_section = lax.axis_index("section")
    my_tensor = lax.axis_index("tensor")
    failed = failed_replica[my_section, my_tensor]
    my_spans = resend_spans[my_section]
    own_weight = weight[0, 0]
    own_first = first_moment[0, 0]
    own_second = second_moment[0, 0]
    rows, width = own_weight.shape
    nchunk = width // 128
    is_failed = my_replica == failed
    part = rows // PLANE

    local = activations[0, 0]
    tokens, cols = local.shape
    squares = jnp.sum(jnp.square(local.astype(WIDE)), axis=1).reshape(-1, 128)
    squares = from_behind(squares, "section", 1).reshape(1, tokens)
    incoming = from_behind(local, "section", 1)
    x = incoming.astype(WIDE)

    mask = serve(failed_replica, resend_spans, own_weight, own_first, own_second)
    served = jnp.sum(exchange_x(mask).astype(WIDE), axis=0).astype(SHORT)

    high, low = two_halves(squares)
    extra = jnp.concatenate([high, low, jnp.zeros((6, tokens), SHORT)], axis=0)
    held = jnp.concatenate([tied(key_grads[0, 0].T, mask), extra], axis=0)
    held = doubled(doubled(held, my_tensor, 0), my_tensor, 1)
    held, served = lax.optimization_barrier((held, served))
    cross = width - my_spans.shape[0] * SPAN
    crossed = served[:, :, :cross] + swap(served[:, :, :cross], "replica", PLANE)
    fresh = jnp.concatenate([crossed, served[:, :, cross:]], axis=2)
    fresh_weight = [fresh[0]] + [swap(fresh[0], "replica", bit) for bit in (1, 2, 3)]
    held = doubled(held, my_tensor, 2).reshape(8, -1, tokens)
    kg_all = held[:, :rows].reshape(8 * rows, tokens)
    squares = jnp.sum(held[:, rows].astype(WIDE) + held[:, rows + 1].astype(WIDE), axis=0)
    inverse_rms = 1.0 / jnp.sqrt(squares / width + 1e-05)

    normed = (x * inverse_rms[:, None]).astype(SHORT)
    grad = lax.dot_general(kg_all, normed, (((1,), (0,)), ((), ())), preferred_element_type=WIDE).astype(SHORT)
    grad = grad.reshape(8, PLANE, part, cols).transpose(1, 0, 2, 3)
    grad = jnp.sum(exchange_x(grad).astype(WIDE), axis=0).astype(SHORT)
    grad = ((grad.astype(WIDE) + swap(grad, "replica", PLANE).astype(WIDE)) / copies).astype(SHORT)

    sent, restored_weight = assemble(failed_replica, resend_spans, own_weight, fresh_weight, grad)
    own_first, own_second, restored_weight, fresh = lax.optimization_barrier((own_first, own_second, restored_weight, fresh))
    got = lax.all_to_all(sent, "tensor", 0, 0, tiled=True)
    weight_cols = got[:, :rows].reshape(8 * rows, cols)
    mean_rows = got[:, rows:].transpose(1, 0, 2).reshape(part, width)

    keys = lax.dot_general(weight_cols, normed, (((1,), (1,)), ((), ())), preferred_element_type=WIDE).astype(SHORT)
    feature = lax.dot_general(kg_all, weight_cols, (((0,), (0,)), ((), ())), preferred_element_type=WIDE)
    product = jnp.sum(feature * x, axis=1).reshape(-1, 128)
    for bit in (1, 2, 4):
        product = product + swap(product, "tensor", bit)
    product = product.reshape(tokens, 1)
    scale = inverse_rms[:, None]
    input_grad = scale * feature - scale * scale * scale * x * product / width
    outgoing = from_behind(input_grad.astype(SHORT), "section", -1)
    got = lax.all_to_all(keys.reshape(8, rows, tokens), "tensor", 0, 0, tiled=True)
    key_out = jnp.sum(got.astype(WIDE), axis=0).T.astype(SHORT)

    def checksum(source):
        shaped = source.reshape(-1, nchunk, 128)
        mixed = jnp.einsum("jnc,cp->jnp", shaped, probe_matrix, precision=lax.Precision.HIGHEST)
        return mixed.reshape(-1, nchunk * probe_matrix.shape[1])

    fresh = unpack(resend_spans, fresh[1:]).astype(WIDE)
    fresh_update = adam(fresh[0], fresh[1], mean_rows.astype(WIDE)).astype(SHORT)
    fresh_sums = checksum(fresh.reshape(2 * part, width)).astype(SHORT).reshape(2, width)
    shared = gather_x(jnp.concatenate([mean_rows, fresh_update, fresh_sums], axis=0))
    mean_grad = shared[:, :part].reshape(rows, width).astype(WIDE)
    fresh_update = shared[:, part : 2 * part].reshape(rows, width).astype(WIDE)
    fresh_sums = shared[:, 2 * part :].reshape(PLANE, 2, part, -1).transpose(1, 0, 2, 3).reshape(2, rows, -1).astype(WIDE)
    update = jnp.where(is_failed, fresh_update, adam(own_first, own_second, mean_grad))
    own_sums = jnp.stack([checksum(own_first), checksum(own_second)])
    checksums = jnp.where(is_failed, fresh_sums, own_sums)
    weight_checksums = checksum(restored_weight.astype(WIDE))
    return (key_out[None, None], outgoing[None, None], update[None, None], checksums[None, None], weight_checksums[None, None])


def solution(mesh):
    by_rows = P("replica", "section", "tensor", None)
    by_features = P("replica", "section", None, "tensor")
    return jax.shard_map(
        shards,
        mesh=mesh,
        in_specs=(by_features, by_features, by_rows, by_rows, by_rows, P(), P(), P()),
        out_specs=(by_features, by_features, by_rows, P("replica", "section", None, "tensor", None), by_rows),
        check_vma=False,
    )
```

```python
import jax
import jax.numpy as jnp
from jax import lax
from jax.experimental import pallas as pl
from jax.experimental.pallas import tpu as pltpu
from jax.sharding import PartitionSpec as P

SHORT = jnp.bfloat16
WIDE = jnp.float32
PLANE = 4
SPAN = 128


def from_behind(block, axis, distance):
    n = lax.axis_size(axis)
    return lax.ppermute(block, axis, [((i - distance) % n, i) for i in range(n)])


def swap(block, axis, bit):
    return lax.ppermute(block, axis, [(i, i ^ bit) for i in range(lax.axis_size(axis))])


def exchange_x(block):
    groups = [[0, 1, 2, 3], [4, 5, 6, 7]]
    return lax.all_to_all(block, "replica", 0, 0, axis_index_groups=groups, tiled=True)


def two_halves(value):
    high = value.astype(SHORT)
    return high, (value - high.astype(WIDE)).astype(SHORT)


def doubled(held, mine, axis):
    bit = 4 >> axis
    came = swap(held, "tensor", bit)
    high = (mine & bit) != 0
    return jnp.stack([jnp.where(high, came, held), jnp.where(high, held, came)], axis=axis)


def gather_x(block):
    groups = [[0, 1, 2, 3], [4, 5, 6, 7]]
    return lax.all_gather(block, "replica", axis=0, tiled=True, axis_index_groups=groups)


def tied(value, *after):
    return lax.optimization_barrier((value,) + after)[0]


def places(spans_ref, section, count):
    ahead = [jnp.int32(0), jnp.int32(count - spans_ref.shape[1])]
    found = []
    for n in range(count):
        listed = spans_ref[section, 0] == n
        for j in range(1, spans_ref.shape[1]):
            listed = listed | (spans_ref[section, j] == n)
        bit = listed.astype(jnp.int32)
        slot = jnp.where(listed, ahead[1], ahead[0])
        found.append((listed, pl.ds(pl.multiple_of(slot * SPAN, SPAN), SPAN)))
        ahead = [ahead[0] + 1 - bit, ahead[1] + bit]
    return found


def serve_kernel(failed_ref, spans_ref, weight_ref, first_ref, second_ref, out_ref):
    section = lax.axis_index("section")
    me = lax.axis_index("replica")
    failed = failed_ref[section, lax.axis_index("tensor")]
    is_primary = (failed ^ PLANE) == me
    is_second = (failed ^ 1) == me
    part = out_ref.shape[2]
    for n, (listed, place) in enumerate(places(spans_ref, section, weight_ref.shape[1] // SPAN)):
        take = (listed & is_second) | (jnp.logical_not(listed) & is_primary)
        for k, ref in enumerate((weight_ref, first_ref, second_ref)):
            for x in range(PLANE):
                block = ref[x * part : (x + 1) * part, n * SPAN : (n + 1) * SPAN].astype(SHORT)
                out_ref[x, k, :, place] = jnp.where(take, block, jnp.zeros_like(block))


def serve(failed, spans, weight, first, second):
    rows, width = weight.shape
    return pl.pallas_call(
        serve_kernel,
        out_shape=jax.ShapeDtypeStruct((PLANE, 3, rows // PLANE, width), SHORT),
        in_specs=[pl.BlockSpec(memory_space=pltpu.SMEM)] * 2 + [pl.BlockSpec(memory_space=pltpu.VMEM)] * 3,
        out_specs=pl.BlockSpec(memory_space=pltpu.VMEM),
        name="serve",
    )(failed, spans, weight, first, second)


def unpack_kernel(spans_ref, placed_ref, out_ref):
    section = lax.axis_index("section")
    for n, (_, place) in enumerate(places(spans_ref, section, out_ref.shape[2] // SPAN)):
        for k in range(out_ref.shape[0]):
            out_ref[k, :, n * SPAN : (n + 1) * SPAN] = placed_ref[k, :, place]


def unpack(spans, placed):
    return pl.pallas_call(
        unpack_kernel,
        out_shape=jax.ShapeDtypeStruct(placed.shape, placed.dtype),
        in_specs=[pl.BlockSpec(memory_space=pltpu.SMEM), pl.BlockSpec(memory_space=pltpu.VMEM)],
        out_specs=pl.BlockSpec(memory_space=pltpu.VMEM),
        name="unpack",
    )(spans, placed)


def assemble_kernel(failed_ref, spans_ref, own_ref, fresh0_ref, fresh1_ref, fresh2_ref, fresh3_ref, grads_ref, sent_ref, restored_ref):
    section = lax.axis_index("section")
    me = lax.axis_index("replica")
    here = failed_ref[section, lax.axis_index("tensor")] == me
    rows, width = own_ref.shape
    groups, _, cols = sent_ref.shape
    part = fresh0_ref.shape[0]
    apart = cols // SPAN
    spans = places(spans_ref, section, width // SPAN)
    for k, fresh_ref in enumerate((fresh0_ref, fresh1_ref, fresh2_ref, fresh3_ref)):
        at = pl.ds(pl.multiple_of(((me & 3) ^ k) * part, part), part)
        for n, (_, place) in enumerate(spans):
            block = jnp.where(here, fresh_ref[:, place], own_ref[at, n * SPAN : (n + 1) * SPAN])
            restored_ref[at, n * SPAN : (n + 1) * SPAN] = block
            sent_ref[n // apart, at, (n % apart) * SPAN : (n % apart + 1) * SPAN] = block
    for t in range(groups):
        sent_ref[t, rows:, :] = grads_ref[t]


def assemble(failed, spans, own, fresh, grads):
    rows, width = own.shape
    groups, part, cols = grads.shape
    return pl.pallas_call(
        assemble_kernel,
        out_shape=(
            jax.ShapeDtypeStruct((groups, rows + part, cols), SHORT),
            jax.ShapeDtypeStruct((rows, width), SHORT),
        ),
        in_specs=[pl.BlockSpec(memory_space=pltpu.SMEM)] * 2 + [pl.BlockSpec(memory_space=pltpu.VMEM)] * 6,
        out_specs=(pl.BlockSpec(memory_space=pltpu.VMEM),) * 2,
        name="assemble",
    )(failed, spans, own, *fresh, grads)


def adam(first, second, grad):
    one = 0.9 * first + 0.1 * grad
    two = 0.95 * second + 0.05 * (grad * grad)
    return one / (jnp.sqrt(two) + 1e-08)


def shards(activations, key_grads, weight, first_moment, second_moment, probe_matrix, failed_replica, resend_spans):
    copies = lax.axis_size("replica")
    my_replica = lax.axis_index("replica")
    my_section = lax.axis_index("section")
    my_tensor = lax.axis_index("tensor")
    failed = failed_replica[my_section, my_tensor]
    my_spans = resend_spans[my_section]
    own_weight = weight[0, 0]
    own_first = first_moment[0, 0]
    own_second = second_moment[0, 0]
    rows, width = own_weight.shape
    nchunk = width // 128
    is_failed = my_replica == failed
    part = rows // PLANE

    local = activations[0, 0]
    tokens, cols = local.shape
    squares = jnp.sum(jnp.square(local.astype(WIDE)), axis=1).reshape(-1, 128)
    squares = from_behind(squares, "section", 1).reshape(1, tokens)
    incoming = from_behind(local, "section", 1)
    x = incoming.astype(WIDE)

    mask = serve(failed_replica, resend_spans, own_weight, own_first, own_second)
    served = jnp.sum(exchange_x(mask).astype(WIDE), axis=0).astype(SHORT)

    high, low = two_halves(squares)
    extra = jnp.concatenate([high, low, jnp.zeros((6, tokens), SHORT)], axis=0)
    held = jnp.concatenate([tied(key_grads[0, 0].T, mask), extra], axis=0)
    held = doubled(doubled(held, my_tensor, 0), my_tensor, 1)
    held, served = lax.optimization_barrier((held, served))
    cross = width - my_spans.shape[0] * SPAN
    crossed = served[:, :, :cross] + swap(served[:, :, :cross], "replica", PLANE)
    fresh = jnp.concatenate([crossed, served[:, :, cross:]], axis=2)
    fresh_weight = [fresh[0]] + [swap(fresh[0], "replica", bit) for bit in (1, 2, 3)]
    held = doubled(held, my_tensor, 2).reshape(8, -1, tokens)
    kg_all = held[:, :rows].reshape(8 * rows, tokens)
    squares = jnp.sum(held[:, rows].astype(WIDE) + held[:, rows + 1].astype(WIDE), axis=0)
    inverse_rms = 1.0 / jnp.sqrt(squares / width + 1e-05)

    normed = (x * inverse_rms[:, None]).astype(SHORT)
    grad = lax.dot_general(kg_all, normed, (((1,), (0,)), ((), ())), preferred_element_type=WIDE).astype(SHORT)
    grad = grad.reshape(8, PLANE, part, cols).transpose(1, 0, 2, 3)
    grad = jnp.sum(exchange_x(grad).astype(WIDE), axis=0).astype(SHORT)
    grad = ((grad.astype(WIDE) + swap(grad, "replica", PLANE).astype(WIDE)) / copies).astype(SHORT)

    sent, restored_weight = assemble(failed_replica, resend_spans, own_weight, fresh_weight, grad)
    own_first, own_second, restored_weight, fresh = lax.optimization_barrier((own_first, own_second, restored_weight, fresh))
    got = lax.all_to_all(sent, "tensor", 0, 0, tiled=True)
    weight_cols = got[:, :rows].reshape(8 * rows, cols)
    mean_rows = got[:, rows:].transpose(1, 0, 2).reshape(part, width)

    keys = lax.dot_general(weight_cols, normed, (((1,), (1,)), ((), ())), preferred_element_type=WIDE).astype(SHORT)
    feature = lax.dot_general(kg_all, weight_cols, (((0,), (0,)), ((), ())), preferred_element_type=WIDE)
    product = jnp.sum(feature * x, axis=1).reshape(-1, 128)
    for bit in (1, 2, 4):
        product = product + swap(product, "tensor", bit)
    product = product.reshape(tokens, 1)
    scale = inverse_rms[:, None]
    input_grad = scale * feature - scale * scale * scale * x * product / width
    outgoing = from_behind(input_grad.astype(SHORT), "section", -1)
    got = lax.all_to_all(keys.reshape(8, rows, tokens), "tensor", 0, 0, tiled=True)
    key_out = jnp.sum(got.astype(WIDE), axis=0).T.astype(SHORT)

    def checksum(source):
        shaped = source.reshape(-1, nchunk, 128)
        mixed = jnp.einsum("jnc,cp->jnp", shaped, probe_matrix, precision=lax.Precision.HIGHEST)
        return mixed.reshape(-1, nchunk * probe_matrix.shape[1])

    fresh = unpack(resend_spans, fresh[1:]).astype(WIDE)
    fresh_update = adam(fresh[0], fresh[1], mean_rows.astype(WIDE)).astype(SHORT)
    fresh_sums = checksum(fresh.reshape(2 * part, width)).astype(SHORT).reshape(2, width)
    mean_grad = gather_x(mean_rows).astype(WIDE)
    fresh_update = gather_x(fresh_update).astype(WIDE)
    fresh_sums = gather_x(fresh_sums).reshape(PLANE, 2, part, -1).transpose(1, 0, 2, 3).reshape(2, rows, -1).astype(WIDE)
    update = jnp.where(is_failed, fresh_update, adam(own_first, own_second, mean_grad))
    own_sums = jnp.stack([checksum(own_first), checksum(own_second)])
    checksums = jnp.where(is_failed, fresh_sums, own_sums)
    weight_checksums = checksum(restored_weight.astype(WIDE))
    return (key_out[None, None], outgoing[None, None], update[None, None], checksums[None, None], weight_checksums[None, None])


def solution(mesh):
    by_rows = P("replica", "section", "tensor", None)
    by_features = P("replica", "section", None, "tensor")
    return jax.shard_map(
        shards,
        mesh=mesh,
        in_specs=(by_features, by_features, by_rows, by_rows, by_rows, P(), P(), P()),
        out_specs=(by_features, by_features, by_rows, P("replica", "section", None, "tensor", None), by_rows),
        check_vma=False,
    )
```

```python
import jax
import jax.numpy as jnp
from jax import lax
from jax.experimental import pallas as pl
from jax.experimental.pallas import tpu as pltpu
from jax.sharding import PartitionSpec as P

SHORT = jnp.bfloat16
WIDE = jnp.float32
PLANE = 4
SPAN = 128


def from_behind(block, axis, distance):
    n = lax.axis_size(axis)
    return lax.ppermute(block, axis, [((i - distance) % n, i) for i in range(n)])


def swap(block, axis, bit):
    return lax.ppermute(block, axis, [(i, i ^ bit) for i in range(lax.axis_size(axis))])


def exchange_x(block):
    groups = [[0, 1, 2, 3], [4, 5, 6, 7]]
    return lax.all_to_all(block, "replica", 0, 0, axis_index_groups=groups, tiled=True)


def two_halves(value):
    high = value.astype(SHORT)
    return high, (value - high.astype(WIDE)).astype(SHORT)


def doubled(held, mine, axis):
    bit = 4 >> axis
    came = swap(held, "tensor", bit)
    high = (mine & bit) != 0
    return jnp.stack([jnp.where(high, came, held), jnp.where(high, held, came)], axis=axis)


def gather_x(block):
    groups = [[0, 1, 2, 3], [4, 5, 6, 7]]
    return lax.all_gather(block, "replica", axis=0, tiled=True, axis_index_groups=groups)


def tied(value, *after):
    return lax.optimization_barrier((value,) + after)[0]


def places(spans_ref, section, count):
    ahead = [jnp.int32(0), jnp.int32(count - spans_ref.shape[1])]
    found = []
    for n in range(count):
        listed = spans_ref[section, 0] == n
        for j in range(1, spans_ref.shape[1]):
            listed = listed | (spans_ref[section, j] == n)
        bit = listed.astype(jnp.int32)
        slot = jnp.where(listed, ahead[1], ahead[0])
        found.append((listed, pl.ds(pl.multiple_of(slot * SPAN, SPAN), SPAN)))
        ahead = [ahead[0] + 1 - bit, ahead[1] + bit]
    return found


def serve_kernel(failed_ref, spans_ref, weight_ref, first_ref, second_ref, out_ref):
    section = lax.axis_index("section")
    me = lax.axis_index("replica")
    failed = failed_ref[section, lax.axis_index("tensor")]
    is_primary = (failed ^ PLANE) == me
    is_second = (failed ^ 1) == me
    part = out_ref.shape[2]
    for n, (listed, place) in enumerate(places(spans_ref, section, weight_ref.shape[1] // SPAN)):
        take = (listed & is_second) | (jnp.logical_not(listed) & is_primary)
        for k, ref in enumerate((weight_ref, first_ref, second_ref)):
            for x in range(PLANE):
                block = ref[x * part : (x + 1) * part, n * SPAN : (n + 1) * SPAN].astype(SHORT)
                out_ref[x, k, :, place] = jnp.where(take, block, jnp.zeros_like(block))


def serve(failed, spans, weight, first, second):
    rows, width = weight.shape
    return pl.pallas_call(
        serve_kernel,
        out_shape=jax.ShapeDtypeStruct((PLANE, 3, rows // PLANE, width), SHORT),
        in_specs=[pl.BlockSpec(memory_space=pltpu.SMEM)] * 2 + [pl.BlockSpec(memory_space=pltpu.VMEM)] * 3,
        out_specs=pl.BlockSpec(memory_space=pltpu.VMEM),
        name="serve",
    )(failed, spans, weight, first, second)


def unpack_kernel(spans_ref, placed_ref, out_ref):
    section = lax.axis_index("section")
    for n, (_, place) in enumerate(places(spans_ref, section, out_ref.shape[2] // SPAN)):
        for k in range(out_ref.shape[0]):
            out_ref[k, :, n * SPAN : (n + 1) * SPAN] = placed_ref[k, :, place]


def unpack(spans, placed):
    return pl.pallas_call(
        unpack_kernel,
        out_shape=jax.ShapeDtypeStruct(placed.shape, placed.dtype),
        in_specs=[pl.BlockSpec(memory_space=pltpu.SMEM), pl.BlockSpec(memory_space=pltpu.VMEM)],
        out_specs=pl.BlockSpec(memory_space=pltpu.VMEM),
        name="unpack",
    )(spans, placed)


def assemble_kernel(failed_ref, spans_ref, own_ref, fresh0_ref, fresh1_ref, fresh2_ref, fresh3_ref, grads_ref, sent_ref, restored_ref):
    section = lax.axis_index("section")
    me = lax.axis_index("replica")
    here = failed_ref[section, lax.axis_index("tensor")] == me
    rows, width = own_ref.shape
    groups, _, cols = sent_ref.shape
    part = fresh0_ref.shape[0]
    apart = cols // SPAN
    spans = places(spans_ref, section, width // SPAN)
    for k, fresh_ref in enumerate((fresh0_ref, fresh1_ref, fresh2_ref, fresh3_ref)):
        at = pl.ds(pl.multiple_of(((me & 3) ^ k) * part, part), part)
        for n, (_, place) in enumerate(spans):
            block = jnp.where(here, fresh_ref[:, place], own_ref[at, n * SPAN : (n + 1) * SPAN])
            restored_ref[at, n * SPAN : (n + 1) * SPAN] = block
            sent_ref[n // apart, at, (n % apart) * SPAN : (n % apart + 1) * SPAN] = block
    for t in range(groups):
        total = grads_ref[0, t].astype(WIDE)
        for x in range(1, PLANE):
            total = total + grads_ref[x, t].astype(WIDE)
        sent_ref[t, rows:, :] = total.astype(SHORT)


def assemble(failed, spans, own, fresh, grads):
    rows, width = own.shape
    _, groups, part, cols = grads.shape
    return pl.pallas_call(
        assemble_kernel,
        out_shape=(
            jax.ShapeDtypeStruct((groups, rows + part, cols), SHORT),
            jax.ShapeDtypeStruct((rows, width), SHORT),
        ),
        in_specs=[pl.BlockSpec(memory_space=pltpu.SMEM)] * 2 + [pl.BlockSpec(memory_space=pltpu.VMEM)] * 6,
        out_specs=(pl.BlockSpec(memory_space=pltpu.VMEM),) * 2,
        name="assemble",
    )(failed, spans, own, *fresh, grads)


def adam(first, second, grad):
    one = 0.9 * first + 0.1 * grad
    two = 0.95 * second + 0.05 * (grad * grad)
    return one / (jnp.sqrt(two) + 1e-08)


def shards(activations, key_grads, weight, first_moment, second_moment, probe_matrix, failed_replica, resend_spans):
    copies = lax.axis_size("replica")
    my_replica = lax.axis_index("replica")
    my_section = lax.axis_index("section")
    my_tensor = lax.axis_index("tensor")
    failed = failed_replica[my_section, my_tensor]
    my_spans = resend_spans[my_section]
    own_weight = weight[0, 0]
    own_first = first_moment[0, 0]
    own_second = second_moment[0, 0]
    rows, width = own_weight.shape
    nchunk = width // 128
    is_failed = my_replica == failed
    part = rows // PLANE

    local = activations[0, 0]
    tokens, cols = local.shape
    squares = jnp.sum(jnp.square(local.astype(WIDE)), axis=1).reshape(-1, 128)
    squares = from_behind(squares, "section", 1).reshape(1, tokens)
    incoming = from_behind(local, "section", 1)
    x = incoming.astype(WIDE)

    mask = serve(failed_replica, resend_spans, own_weight, own_first, own_second)
    served = jnp.sum(exchange_x(mask).astype(WIDE), axis=0).astype(SHORT)

    high, low = two_halves(squares)
    extra = jnp.concatenate([high, low, jnp.zeros((6, tokens), SHORT)], axis=0)
    held = jnp.concatenate([tied(key_grads[0, 0].T, mask), extra], axis=0)
    held = doubled(doubled(held, my_tensor, 0), my_tensor, 1)
    held, served = lax.optimization_barrier((held, served))
    cross = width - my_spans.shape[0] * SPAN
    crossed = served[:, :, :cross] + swap(served[:, :, :cross], "replica", PLANE)
    fresh = jnp.concatenate([crossed, served[:, :, cross:]], axis=2)
    fresh_weight = [fresh[0]] + [swap(fresh[0], "replica", bit) for bit in (1, 2, 3)]
    held = doubled(held, my_tensor, 2).reshape(8, -1, tokens)
    kg_all = held[:, :rows].reshape(8 * rows, tokens)
    squares = jnp.sum(held[:, rows].astype(WIDE) + held[:, rows + 1].astype(WIDE), axis=0)
    inverse_rms = 1.0 / jnp.sqrt(squares / width + 1e-05)

    normed = (x * inverse_rms[:, None]).astype(SHORT)
    grad = lax.dot_general(kg_all, normed, (((1,), (0,)), ((), ())), preferred_element_type=WIDE).astype(SHORT)
    grad = grad.reshape(8, PLANE, part, cols).transpose(1, 0, 2, 3)
    grad = exchange_x(grad)

    sent, restored_weight = assemble(failed_replica, resend_spans, own_weight, fresh_weight, grad)
    own_first, own_second, restored_weight, fresh = lax.optimization_barrier((own_first, own_second, restored_weight, fresh))
    got = lax.all_to_all(sent, "tensor", 0, 0, tiled=True)
    weight_cols = got[:, :rows].reshape(8 * rows, cols)
    grad_rows = got[:, rows:].transpose(1, 0, 2).reshape(part, width)
    mean_rows = (grad_rows.astype(WIDE) + swap(grad_rows, "replica", PLANE).astype(WIDE)) / copies

    keys = lax.dot_general(weight_cols, normed, (((1,), (1,)), ((), ())), preferred_element_type=WIDE).astype(SHORT)
    feature = lax.dot_general(kg_all, weight_cols, (((0,), (0,)), ((), ())), preferred_element_type=WIDE)
    product = jnp.sum(feature * x, axis=1).reshape(1, -1, 128)
    product = lax.all_to_all(jnp.broadcast_to(product, (8,) + product.shape[1:]), "tensor", 0, 0, tiled=True)
    product = jnp.sum(product, axis=0).reshape(tokens, 1)
    product, keys = lax.optimization_barrier((product, keys))
    scale = inverse_rms[:, None]
    input_grad = scale * feature - scale * scale * scale * x * product / width
    outgoing = from_behind(input_grad.astype(SHORT), "section", -1)
    got = lax.all_to_all(keys.reshape(8, rows, tokens), "tensor", 0, 0, tiled=True)
    key_out = jnp.sum(got.astype(WIDE), axis=0).T.astype(SHORT)

    def checksum(source):
        shaped = source.reshape(-1, nchunk, 128)
        mixed = jnp.einsum("jnc,cp->jnp", shaped, probe_matrix, precision=lax.Precision.HIGHEST)
        return mixed.reshape(-1, nchunk * probe_matrix.shape[1])

    fresh = unpack(resend_spans, fresh[1:]).astype(WIDE)
    fresh_update = adam(fresh[0], fresh[1], mean_rows).astype(SHORT)
    fresh_sums = checksum(fresh.reshape(2 * part, width)).astype(SHORT).reshape(2, width)
    mean_grad = gather_x(mean_rows.astype(SHORT)).astype(WIDE)
    fresh_update = gather_x(fresh_update).astype(WIDE)
    fresh_sums = gather_x(fresh_sums).reshape(PLANE, 2, part, -1).transpose(1, 0, 2, 3).reshape(2, rows, -1).astype(WIDE)
    update = jnp.where(is_failed, fresh_update, adam(own_first, own_second, mean_grad))
    own_sums = jnp.stack([checksum(own_first), checksum(own_second)])
    checksums = jnp.where(is_failed, fresh_sums, own_sums)
    weight_checksums = checksum(restored_weight.astype(WIDE))
    return (key_out[None, None], outgoing[None, None], update[None, None], checksums[None, None], weight_checksums[None, None])


def solution(mesh):
    by_rows = P("replica", "section", "tensor", None)
    by_features = P("replica", "section", None, "tensor")
    return jax.shard_map(
        shards,
        mesh=mesh,
        in_specs=(by_features, by_features, by_rows, by_rows, by_rows, P(), P(), P()),
        out_specs=(by_features, by_features, by_rows, P("replica", "section", None, "tensor", None), by_rows),
        check_vma=False,
    )
```

```python
import jax
import jax.numpy as jnp
from jax import lax
from jax.experimental import pallas as pl
from jax.experimental.pallas import tpu as pltpu
from jax.sharding import PartitionSpec as P

SHORT = jnp.bfloat16
WIDE = jnp.float32
PLANE = 4
SPAN = 128


def from_behind(block, axis, distance):
    n = lax.axis_size(axis)
    return lax.ppermute(block, axis, [((i - distance) % n, i) for i in range(n)])


def swap(block, axis, bit):
    return lax.ppermute(block, axis, [(i, i ^ bit) for i in range(lax.axis_size(axis))])


def exchange_x(block):
    groups = [[0, 1, 2, 3], [4, 5, 6, 7]]
    return lax.all_to_all(block, "replica", 0, 0, axis_index_groups=groups, tiled=True)


def two_halves(value):
    high = value.astype(SHORT)
    return high, (value - high.astype(WIDE)).astype(SHORT)


def in_order(held, mine, bits):
    for bit in bits:
        split = held.reshape((held.shape[0] // (2 * bit), 2, bit) + held.shape[1:])
        held = jnp.where((mine & bit) != 0, split[:, ::-1], split).reshape(held.shape)
    return held


def doubled(held, mine, axis, part=None):
    bit = 4 >> axis
    sent = held
    if part is not None:
        high, low = two_halves(part)
        rows = held.reshape(-1, held.shape[-1])
        sent = jnp.concatenate([rows, high, low, jnp.zeros((6, held.shape[-1]), SHORT)], axis=0)
    came = swap(sent, "tensor", bit)
    if part is not None:
        part = part + came[-8:-7].astype(WIDE) + came[-7:-6].astype(WIDE)
        came = came[:-8].reshape(held.shape)
    upper = (mine & bit) != 0
    held = jnp.stack([jnp.where(upper, came, held), jnp.where(upper, held, came)], axis=axis)
    return held if part is None else (held, part)


def gather_x(block):
    held = jnp.stack([block] + [swap(block, "replica", bit) for bit in (1, 2, 3)])
    return in_order(held, lax.axis_index("replica") & 3, (2, 1))


def broadcast_x(block):
    return exchange_x(jnp.broadcast_to(block[None], (PLANE,) + block.shape))


def tied(value, *after):
    return lax.optimization_barrier((value,) + after)[0]


def places(spans_ref, section, count):
    ahead = [jnp.int32(0), jnp.int32(count - spans_ref.shape[1])]
    found = []
    for n in range(count):
        listed = spans_ref[section, 0] == n
        for j in range(1, spans_ref.shape[1]):
            listed = listed | (spans_ref[section, j] == n)
        bit = listed.astype(jnp.int32)
        slot = jnp.where(listed, ahead[1], ahead[0])
        found.append((listed, pl.ds(pl.multiple_of(slot * SPAN, SPAN), SPAN)))
        ahead = [ahead[0] + 1 - bit, ahead[1] + bit]
    return found


def serve_kernel(failed_ref, spans_ref, weight_ref, first_ref, second_ref, weight_out_ref, moments_out_ref):
    section = lax.axis_index("section")
    me = lax.axis_index("replica")
    failed = failed_ref[section, lax.axis_index("tensor")]
    is_primary = (failed ^ PLANE) == me
    is_second = (failed ^ 1) == me
    part = weight_out_ref.shape[1]
    for n, (listed, place) in enumerate(places(spans_ref, section, weight_ref.shape[1] // SPAN)):
        take = (listed & is_second) | (jnp.logical_not(listed) & is_primary)
        here = pl.ds(n * SPAN, SPAN)
        for x in range(PLANE):
            at = pl.ds(x * part, part)
            block = weight_ref[at, here]
            weight_out_ref[x, :, place] = jnp.where(take, block, jnp.zeros_like(block))
            for k, ref in enumerate((first_ref, second_ref)):
                block = ref[at, here].astype(SHORT)
                moments_out_ref[x, k, :, place] = jnp.where(take, block, jnp.zeros_like(block))


def serve(failed, spans, weight, first, second):
    rows, width = weight.shape
    return pl.pallas_call(
        serve_kernel,
        out_shape=(
            jax.ShapeDtypeStruct((PLANE, rows // PLANE, width), SHORT),
            jax.ShapeDtypeStruct((PLANE, 2, rows // PLANE, width), SHORT),
        ),
        in_specs=[pl.BlockSpec(memory_space=pltpu.SMEM)] * 2 + [pl.BlockSpec(memory_space=pltpu.VMEM)] * 3,
        out_specs=(pl.BlockSpec(memory_space=pltpu.VMEM),) * 2,
        name="serve",
    )(failed, spans, weight, first, second)


def unpack_kernel(spans_ref, placed_ref, out_ref):
    section = lax.axis_index("section")
    for n, (_, place) in enumerate(places(spans_ref, section, out_ref.shape[2] // SPAN)):
        for k in range(out_ref.shape[0]):
            out_ref[k, :, n * SPAN : (n + 1) * SPAN] = placed_ref[k, :, place]


def unpack(spans, placed):
    return pl.pallas_call(
        unpack_kernel,
        out_shape=jax.ShapeDtypeStruct(placed.shape, placed.dtype),
        in_specs=[pl.BlockSpec(memory_space=pltpu.SMEM), pl.BlockSpec(memory_space=pltpu.VMEM)],
        out_specs=pl.BlockSpec(memory_space=pltpu.VMEM),
        name="unpack",
    )(spans, placed)


def assemble_kernel(failed_ref, spans_ref, own_ref, fresh0_ref, fresh1_ref, fresh2_ref, fresh3_ref, grads_ref, sent_ref, restored_ref):
    section = lax.axis_index("section")
    me = lax.axis_index("replica")
    here = failed_ref[section, lax.axis_index("tensor")] == me
    rows, width = own_ref.shape
    groups, _, cols = sent_ref.shape
    part = fresh0_ref.shape[0]
    apart = cols // SPAN
    spans = places(spans_ref, section, width // SPAN)
    for k, fresh_ref in enumerate((fresh0_ref, fresh1_ref, fresh2_ref, fresh3_ref)):
        at = pl.ds(pl.multiple_of(((me & 3) ^ k) * part, part), part)
        for n, (_, place) in enumerate(spans):
            block = jnp.where(here, fresh_ref[:, place], own_ref[at, n * SPAN : (n + 1) * SPAN])
            restored_ref[at, n * SPAN : (n + 1) * SPAN] = block
            sent_ref[n // apart, at, (n % apart) * SPAN : (n % apart + 1) * SPAN] = block
    for t in range(groups):
        total = grads_ref[0, t].astype(WIDE)
        for x in range(1, PLANE):
            total = total + grads_ref[x, t].astype(WIDE)
        sent_ref[t, rows:, :] = total.astype(SHORT)


def assemble(failed, spans, own, fresh, grads):
    rows, width = own.shape
    _, groups, part, cols = grads.shape
    return pl.pallas_call(
        assemble_kernel,
        out_shape=(
            jax.ShapeDtypeStruct((groups, rows + part, cols), SHORT),
            jax.ShapeDtypeStruct((rows, width), SHORT),
        ),
        in_specs=[pl.BlockSpec(memory_space=pltpu.SMEM)] * 2 + [pl.BlockSpec(memory_space=pltpu.VMEM)] * 6,
        out_specs=(pl.BlockSpec(memory_space=pltpu.VMEM),) * 2,
        name="assemble",
    )(failed, spans, own, *fresh, grads)


def adam(first, second, grad):
    one = 0.9 * first + 0.1 * grad
    two = 0.95 * second + 0.05 * (grad * grad)
    return one / (jnp.sqrt(two) + 1e-08)


def shards(activations, key_grads, weight, first_moment, second_moment, probe_matrix, failed_replica, resend_spans):
    copies = lax.axis_size("replica")
    my_replica = lax.axis_index("replica")
    my_section = lax.axis_index("section")
    my_tensor = lax.axis_index("tensor")
    failed = failed_replica[my_section, my_tensor]
    my_spans = resend_spans[my_section]
    own_weight = weight[0, 0]
    own_first = first_moment[0, 0]
    own_second = second_moment[0, 0]
    rows, width = own_weight.shape
    nchunk = width // 128
    is_failed = my_replica == failed
    part = rows // PLANE

    local = activations[0, 0]
    tokens, cols = local.shape
    squares = jnp.sum(jnp.square(local.astype(WIDE)), axis=1).reshape(-1, 128)
    squares = from_behind(squares, "section", 1).reshape(1, tokens)
    incoming = from_behind(local, "section", 1)
    x = incoming.astype(WIDE)

    def summed(parts):
        return jnp.sum(parts.astype(WIDE), axis=0).astype(SHORT)

    cross = width - my_spans.shape[0] * SPAN

    def both_planes(served):
        crossed = served[..., :cross] + swap(served[..., :cross], "replica", PLANE)
        return jnp.concatenate([crossed, served[..., cross:]], axis=-1)

    mask_weight, mask_moments = serve(failed_replica, resend_spans, own_weight, own_first, own_second)
    served_weight = summed(exchange_x(mask_weight))

    held = doubled(tied(key_grads[0, 0].T, mask_weight), my_tensor, 0)
    squares = squares + swap(squares, "tensor", 4)
    held, served_weight, mask_moments, squares = lax.optimization_barrier((held, served_weight, mask_moments, squares))
    held, squares = doubled(held, my_tensor, 1, squares)
    held, served_weight, mask_moments = lax.optimization_barrier((held, served_weight, mask_moments))
    served_moments = summed(exchange_x(mask_moments))
    fresh_weight = both_planes(served_weight)
    fresh_weight = [fresh_weight] + [swap(fresh_weight, "replica", bit) for bit in (1, 2, 3)]
    held, squares = doubled(held, my_tensor, 2, squares)
    kg_all = held.reshape(8 * rows, tokens)
    inverse_rms = 1.0 / jnp.sqrt(squares.reshape(tokens) / width + 1e-05)

    normed = (x * inverse_rms[:, None]).astype(SHORT)
    grad = lax.dot_general(kg_all, normed, (((1,), (0,)), ((), ())), preferred_element_type=WIDE).astype(SHORT)
    grad = grad.reshape(8, PLANE, part, cols).transpose(1, 0, 2, 3)
    grad, served_moments = lax.optimization_barrier((grad, served_moments))
    grad = exchange_x(grad)

    sent, restored_weight = assemble(failed_replica, resend_spans, own_weight, fresh_weight, grad)
    own_first, own_second, restored_weight = lax.optimization_barrier((own_first, own_second, restored_weight))
    def checksum(source):
        shaped = source.reshape(-1, nchunk, 128)
        mixed = jnp.einsum("jnc,cp->jnp", shaped, probe_matrix, precision=lax.Precision.HIGHEST)
        return mixed.reshape(-1, nchunk * probe_matrix.shape[1])

    weight_checksums = checksum(restored_weight.astype(WIDE))
    weight_checksums, served_moments = lax.optimization_barrier((weight_checksums, served_moments))
    fresh = both_planes(served_moments)
    got = lax.all_to_all(sent, "tensor", 0, 0, tiled=True)
    weight_cols = got[:, :rows].reshape(8 * rows, cols)
    grad_rows = got[:, rows:].transpose(1, 0, 2).reshape(part, width)
    mean_rows = (grad_rows.astype(WIDE) + swap(grad_rows, "replica", PLANE).astype(WIDE)) / copies

    keys = lax.dot_general(weight_cols, normed, (((1,), (1,)), ((), ())), preferred_element_type=WIDE).astype(SHORT)
    feature = lax.dot_general(kg_all, weight_cols, (((0,), (0,)), ((), ())), preferred_element_type=WIDE)
    product = jnp.sum(feature * x, axis=1).reshape(-1, 128)
    for bit in (1, 2, 4):
        product = product + swap(product, "tensor", bit)
    product = product.reshape(tokens, 1)
    scale = inverse_rms[:, None]
    input_grad = scale * feature - scale * scale * scale * x * product / width
    outgoing = from_behind(input_grad.astype(SHORT), "section", -1)
    got = lax.all_to_all(keys.reshape(8, rows, tokens), "tensor", 0, 0, tiled=True)
    key_out = jnp.sum(got.astype(WIDE), axis=0).T.astype(SHORT)

    fresh = unpack(resend_spans, fresh).astype(WIDE)
    fresh_update = adam(fresh[0], fresh[1], mean_rows).astype(SHORT)
    fresh_sums = checksum(fresh.reshape(2 * part, width)).astype(SHORT).reshape(2, width)
    shared = gather_x(jnp.concatenate([mean_rows.astype(SHORT), fresh_update, fresh_sums], axis=0))
    mean_grad = shared[:, :part].reshape(rows, width).astype(WIDE)
    fresh_update = shared[:, part : 2 * part].reshape(rows, width).astype(WIDE)
    fresh_sums = shared[:, 2 * part :].reshape(PLANE, 2, part, -1).transpose(1, 0, 2, 3).reshape(2, rows, -1).astype(WIDE)
    update = jnp.where(is_failed, fresh_update, adam(own_first, own_second, mean_grad))
    own_sums = jnp.stack([checksum(own_first), checksum(own_second)])
    checksums = jnp.where(is_failed, fresh_sums, own_sums)
    return (key_out[None, None], outgoing[None, None], update[None, None], checksums[None, None], weight_checksums[None, None])


def solution(mesh):
    by_rows = P("replica", "section", "tensor", None)
    by_features = P("replica", "section", None, "tensor")
    return jax.shard_map(
        shards,
        mesh=mesh,
        in_specs=(by_features, by_features, by_rows, by_rows, by_rows, P(), P(), P()),
        out_specs=(by_features, by_features, by_rows, P("replica", "section", None, "tensor", None), by_rows),
        check_vma=False,
    )
```

```python
import jax
import jax.numpy as jnp
from jax import lax
from jax.experimental import pallas as pl
from jax.experimental.pallas import tpu as pltpu
from jax.sharding import PartitionSpec as P

SHORT = jnp.bfloat16
WIDE = jnp.float32
PLANE = 4
SPAN = 128


def from_behind(block, axis, distance):
    n = lax.axis_size(axis)
    return lax.ppermute(block, axis, [((i - distance) % n, i) for i in range(n)])


def swap(block, axis, bit):
    return lax.ppermute(block, axis, [(i, i ^ bit) for i in range(lax.axis_size(axis))])


def exchange_x(block):
    groups = [[0, 1, 2, 3], [4, 5, 6, 7]]
    return lax.all_to_all(block, "replica", 0, 0, axis_index_groups=groups, tiled=True)


def two_halves(value):
    high = value.astype(SHORT)
    return high, (value - high.astype(WIDE)).astype(SHORT)


def in_order(held, mine, bits):
    for bit in bits:
        split = held.reshape((held.shape[0] // (2 * bit), 2, bit) + held.shape[1:])
        held = jnp.where((mine & bit) != 0, split[:, ::-1], split).reshape(held.shape)
    return held


def doubled(held, mine, axis, part=None):
    bit = 4 >> axis
    sent = held
    if part is not None:
        high, low = two_halves(part)
        rows = held.reshape(-1, held.shape[-1])
        sent = jnp.concatenate([rows, high, low, jnp.zeros((6, held.shape[-1]), SHORT)], axis=0)
    came = swap(sent, "tensor", bit)
    if part is not None:
        part = part + came[-8:-7].astype(WIDE) + came[-7:-6].astype(WIDE)
        came = came[:-8].reshape(held.shape)
    upper = (mine & bit) != 0
    held = jnp.stack([jnp.where(upper, came, held), jnp.where(upper, held, came)], axis=axis)
    return held if part is None else (held, part)


def gather_x(block):
    held = jnp.stack([block] + [swap(block, "replica", bit) for bit in (1, 2, 3)])
    return in_order(held, lax.axis_index("replica") & 3, (2, 1))


def broadcast_x(block):
    return exchange_x(jnp.broadcast_to(block[None], (PLANE,) + block.shape))


def tied(value, *after):
    return lax.optimization_barrier((value,) + after)[0]


def places(spans_ref, section, count):
    ahead = [jnp.int32(0), jnp.int32(count - spans_ref.shape[1])]
    found = []
    for n in range(count):
        listed = spans_ref[section, 0] == n
        for j in range(1, spans_ref.shape[1]):
            listed = listed | (spans_ref[section, j] == n)
        bit = listed.astype(jnp.int32)
        slot = jnp.where(listed, ahead[1], ahead[0])
        found.append((listed, pl.ds(pl.multiple_of(slot * SPAN, SPAN), SPAN)))
        ahead = [ahead[0] + 1 - bit, ahead[1] + bit]
    return found


def serve_kernel(failed_ref, spans_ref, weight_ref, first_ref, second_ref, out_ref):
    section = lax.axis_index("section")
    me = lax.axis_index("replica")
    failed = failed_ref[section, lax.axis_index("tensor")]
    is_primary = (failed ^ PLANE) == me
    is_second = (failed ^ 1) == me
    part = out_ref.shape[2]
    for n, (listed, place) in enumerate(places(spans_ref, section, weight_ref.shape[1] // SPAN)):
        take = (listed & is_second) | (jnp.logical_not(listed) & is_primary)
        for k, ref in enumerate((weight_ref, first_ref, second_ref)):
            for x in range(PLANE):
                block = ref[x * part : (x + 1) * part, n * SPAN : (n + 1) * SPAN].astype(SHORT)
                out_ref[x, k, :, place] = jnp.where(take, block, jnp.zeros_like(block))


def serve(failed, spans, weight, first, second):
    rows, width = weight.shape
    return pl.pallas_call(
        serve_kernel,
        out_shape=jax.ShapeDtypeStruct((PLANE, 3, rows // PLANE, width), SHORT),
        in_specs=[pl.BlockSpec(memory_space=pltpu.SMEM)] * 2 + [pl.BlockSpec(memory_space=pltpu.VMEM)] * 3,
        out_specs=pl.BlockSpec(memory_space=pltpu.VMEM),
        name="serve",
    )(failed, spans, weight, first, second)


def unpack_kernel(spans_ref, placed_ref, out_ref):
    section = lax.axis_index("section")
    for n, (_, place) in enumerate(places(spans_ref, section, out_ref.shape[2] // SPAN)):
        for k in range(out_ref.shape[0]):
            out_ref[k, :, n * SPAN : (n + 1) * SPAN] = placed_ref[k, :, place]


def unpack(spans, placed):
    return pl.pallas_call(
        unpack_kernel,
        out_shape=jax.ShapeDtypeStruct(placed.shape, placed.dtype),
        in_specs=[pl.BlockSpec(memory_space=pltpu.SMEM), pl.BlockSpec(memory_space=pltpu.VMEM)],
        out_specs=pl.BlockSpec(memory_space=pltpu.VMEM),
        name="unpack",
    )(spans, placed)


def assemble_kernel(failed_ref, spans_ref, own_ref, fresh0_ref, fresh1_ref, fresh2_ref, fresh3_ref, grads_ref, sent_ref, restored_ref):
    section = lax.axis_index("section")
    me = lax.axis_index("replica")
    here = failed_ref[section, lax.axis_index("tensor")] == me
    rows, width = own_ref.shape
    groups, _, cols = sent_ref.shape
    part = fresh0_ref.shape[0]
    apart = cols // SPAN
    spans = places(spans_ref, section, width // SPAN)
    for k, fresh_ref in enumerate((fresh0_ref, fresh1_ref, fresh2_ref, fresh3_ref)):
        at = pl.ds(pl.multiple_of(((me & 3) ^ k) * part, part), part)
        for n, (_, place) in enumerate(spans):
            block = jnp.where(here, fresh_ref[:, place], own_ref[at, n * SPAN : (n + 1) * SPAN])
            restored_ref[at, n * SPAN : (n + 1) * SPAN] = block
            sent_ref[n // apart, at, (n % apart) * SPAN : (n % apart + 1) * SPAN] = block
    for t in range(groups):
        total = grads_ref[0, t].astype(WIDE)
        for x in range(1, PLANE):
            total = total + grads_ref[x, t].astype(WIDE)
        sent_ref[t, rows:, :] = total.astype(SHORT)


def assemble(failed, spans, own, fresh, grads):
    rows, width = own.shape
    _, groups, part, cols = grads.shape
    return pl.pallas_call(
        assemble_kernel,
        out_shape=(
            jax.ShapeDtypeStruct((groups, rows + part, cols), SHORT),
            jax.ShapeDtypeStruct((rows, width), SHORT),
        ),
        in_specs=[pl.BlockSpec(memory_space=pltpu.SMEM)] * 2 + [pl.BlockSpec(memory_space=pltpu.VMEM)] * 6,
        out_specs=(pl.BlockSpec(memory_space=pltpu.VMEM),) * 2,
        name="assemble",
    )(failed, spans, own, *fresh, grads)


def adam(first, second, grad):
    one = 0.9 * first + 0.1 * grad
    two = 0.95 * second + 0.05 * (grad * grad)
    return one / (jnp.sqrt(two) + 1e-08)


def shards(activations, key_grads, weight, first_moment, second_moment, probe_matrix, failed_replica, resend_spans):
    copies = lax.axis_size("replica")
    my_replica = lax.axis_index("replica")
    my_section = lax.axis_index("section")
    my_tensor = lax.axis_index("tensor")
    failed = failed_replica[my_section, my_tensor]
    my_spans = resend_spans[my_section]
    own_weight = weight[0, 0]
    own_first = first_moment[0, 0]
    own_second = second_moment[0, 0]
    rows, width = own_weight.shape
    nchunk = width // 128
    is_failed = my_replica == failed
    part = rows // PLANE

    local = activations[0, 0]
    tokens, cols = local.shape
    squares = jnp.sum(jnp.square(local.astype(WIDE)), axis=1).reshape(-1, 128)
    squares = from_behind(squares, "section", 1).reshape(1, tokens)
    incoming = from_behind(local, "section", 1)
    x = incoming.astype(WIDE)

    mask = serve(failed_replica, resend_spans, own_weight, own_first, own_second)
    served = jnp.sum(exchange_x(mask).astype(WIDE), axis=0).astype(SHORT)

    held = doubled(tied(key_grads[0, 0].T, mask), my_tensor, 0)
    held, squares = doubled(held, my_tensor, 1, squares)
    held, served = lax.optimization_barrier((held, served))
    cross = width - my_spans.shape[0] * SPAN
    crossed = served[:, :, :cross] + swap(served[:, :, :cross], "replica", PLANE)
    fresh = jnp.concatenate([crossed, served[:, :, cross:]], axis=2)
    fresh_weight = [fresh[0]] + [swap(fresh[0], "replica", bit) for bit in (1, 2, 3)]
    held, squares = doubled(held, my_tensor, 2, squares)
    kg_all = held.reshape(8 * rows, tokens)
    squares = (squares + swap(squares, "tensor", 4)).reshape(tokens)
    inverse_rms = 1.0 / jnp.sqrt(squares / width + 1e-05)

    normed = (x * inverse_rms[:, None]).astype(SHORT)
    grad = lax.dot_general(kg_all, normed, (((1,), (0,)), ((), ())), preferred_element_type=WIDE).astype(SHORT)
    grad = grad.reshape(8, PLANE, part, cols).transpose(1, 0, 2, 3)
    grad = exchange_x(grad)

    sent, restored_weight = assemble(failed_replica, resend_spans, own_weight, fresh_weight, grad)
    own_first, own_second, restored_weight, fresh = lax.optimization_barrier((own_first, own_second, restored_weight, fresh))
    got = lax.all_to_all(sent, "tensor", 0, 0, tiled=True)
    weight_cols = got[:, :rows].reshape(8 * rows, cols)
    grad_rows = got[:, rows:].transpose(1, 0, 2).reshape(part, width)
    mean_rows = (grad_rows.astype(WIDE) + swap(grad_rows, "replica", PLANE).astype(WIDE)) / copies

    keys = lax.dot_general(weight_cols, normed, (((1,), (1,)), ((), ())), preferred_element_type=WIDE).astype(SHORT)
    feature = lax.dot_general(kg_all, weight_cols, (((0,), (0,)), ((), ())), preferred_element_type=WIDE)
    product = jnp.sum(feature * x, axis=1).reshape(-1, 128)
    for bit in (1, 2, 4):
        product = product + swap(product, "tensor", bit)
    product = product.reshape(tokens, 1)
    scale = inverse_rms[:, None]
    input_grad = scale * feature - scale * scale * scale * x * product / width
    outgoing = from_behind(input_grad.astype(SHORT), "section", -1)
    got = lax.all_to_all(keys.reshape(8, rows, tokens), "tensor", 0, 0, tiled=True)
    key_out = jnp.sum(got.astype(WIDE), axis=0).T.astype(SHORT)

    def checksum(source):
        shaped = source.reshape(-1, nchunk, 128)
        mixed = jnp.einsum("jnc,cp->jnp", shaped, probe_matrix, precision=lax.Precision.HIGHEST)
        return mixed.reshape(-1, nchunk * probe_matrix.shape[1])

    fresh = unpack(resend_spans, fresh[1:]).astype(WIDE)
    fresh_update = adam(fresh[0], fresh[1], mean_rows).astype(SHORT)
    fresh_sums = checksum(fresh.reshape(2 * part, width)).astype(SHORT).reshape(2, width)
    shared = gather_x(jnp.concatenate([mean_rows.astype(SHORT), fresh_update, fresh_sums], axis=0))
    mean_grad = shared[:, :part].reshape(rows, width).astype(WIDE)
    fresh_update = shared[:, part : 2 * part].reshape(rows, width).astype(WIDE)
    fresh_sums = shared[:, 2 * part :].reshape(PLANE, 2, part, -1).transpose(1, 0, 2, 3).reshape(2, rows, -1).astype(WIDE)
    update = jnp.where(is_failed, fresh_update, adam(own_first, own_second, mean_grad))
    own_sums = jnp.stack([checksum(own_first), checksum(own_second)])
    checksums = jnp.where(is_failed, fresh_sums, own_sums)
    weight_checksums = checksum(restored_weight.astype(WIDE))
    return (key_out[None, None], outgoing[None, None], update[None, None], checksums[None, None], weight_checksums[None, None])


def solution(mesh):
    by_rows = P("replica", "section", "tensor", None)
    by_features = P("replica", "section", None, "tensor")
    return jax.shard_map(
        shards,
        mesh=mesh,
        in_specs=(by_features, by_features, by_rows, by_rows, by_rows, P(), P(), P()),
        out_specs=(by_features, by_features, by_rows, P("replica", "section", None, "tensor", None), by_rows),
        check_vma=False,
    )
```

```python
import jax
import jax.numpy as jnp
from jax import lax
from jax.experimental import pallas as pl
from jax.experimental.pallas import tpu as pltpu
from jax.sharding import PartitionSpec as P

SHORT = jnp.bfloat16
WIDE = jnp.float32
PLANE = 4
SPAN = 128


def from_behind(block, axis, distance):
    n = lax.axis_size(axis)
    return lax.ppermute(block, axis, [((i - distance) % n, i) for i in range(n)])


def swap(block, axis, bit):
    return lax.ppermute(block, axis, [(i, i ^ bit) for i in range(lax.axis_size(axis))])


def exchange_x(block):
    groups = [[0, 1, 2, 3], [4, 5, 6, 7]]
    return lax.all_to_all(block, "replica", 0, 0, axis_index_groups=groups, tiled=True)


def two_halves(value):
    high = value.astype(SHORT)
    return high, (value - high.astype(WIDE)).astype(SHORT)


def in_order(held, mine, bits):
    for bit in bits:
        split = held.reshape((held.shape[0] // (2 * bit), 2, bit) + held.shape[1:])
        held = jnp.where((mine & bit) != 0, split[:, ::-1], split).reshape(held.shape)
    return held


def doubled(held, mine, axis):
    bit = 4 >> axis
    came = swap(held, "tensor", bit)
    high = (mine & bit) != 0
    return jnp.stack([jnp.where(high, came, held), jnp.where(high, held, came)], axis=axis)


def gather_x(block):
    held = jnp.stack([block] + [swap(block, "replica", bit) for bit in (1, 2, 3)])
    return in_order(held, lax.axis_index("replica") & 3, (2, 1))


def broadcast_x(block):
    return exchange_x(jnp.broadcast_to(block[None], (PLANE,) + block.shape))


def tied(value, *after):
    return lax.optimization_barrier((value,) + after)[0]


def places(spans_ref, section, count):
    ahead = [jnp.int32(0), jnp.int32(count - spans_ref.shape[1])]
    found = []
    for n in range(count):
        listed = spans_ref[section, 0] == n
        for j in range(1, spans_ref.shape[1]):
            listed = listed | (spans_ref[section, j] == n)
        bit = listed.astype(jnp.int32)
        slot = jnp.where(listed, ahead[1], ahead[0])
        found.append((listed, pl.ds(pl.multiple_of(slot * SPAN, SPAN), SPAN)))
        ahead = [ahead[0] + 1 - bit, ahead[1] + bit]
    return found


def serve_kernel(failed_ref, spans_ref, weight_ref, first_ref, second_ref, out_ref):
    section = lax.axis_index("section")
    me = lax.axis_index("replica")
    failed = failed_ref[section, lax.axis_index("tensor")]
    is_primary = (failed ^ PLANE) == me
    is_second = (failed ^ 1) == me
    part = out_ref.shape[2]
    for n, (listed, place) in enumerate(places(spans_ref, section, weight_ref.shape[1] // SPAN)):
        take = (listed & is_second) | (jnp.logical_not(listed) & is_primary)
        for k, ref in enumerate((weight_ref, first_ref, second_ref)):
            for x in range(PLANE):
                block = ref[x * part : (x + 1) * part, n * SPAN : (n + 1) * SPAN].astype(SHORT)
                out_ref[x, k, :, place] = jnp.where(take, block, jnp.zeros_like(block))


def serve(failed, spans, weight, first, second):
    rows, width = weight.shape
    return pl.pallas_call(
        serve_kernel,
        out_shape=jax.ShapeDtypeStruct((PLANE, 3, rows // PLANE, width), SHORT),
        in_specs=[pl.BlockSpec(memory_space=pltpu.SMEM)] * 2 + [pl.BlockSpec(memory_space=pltpu.VMEM)] * 3,
        out_specs=pl.BlockSpec(memory_space=pltpu.VMEM),
        name="serve",
    )(failed, spans, weight, first, second)


def unpack_kernel(spans_ref, placed_ref, out_ref):
    section = lax.axis_index("section")
    for n, (_, place) in enumerate(places(spans_ref, section, out_ref.shape[2] // SPAN)):
        for k in range(out_ref.shape[0]):
            out_ref[k, :, n * SPAN : (n + 1) * SPAN] = placed_ref[k, :, place]


def unpack(spans, placed):
    return pl.pallas_call(
        unpack_kernel,
        out_shape=jax.ShapeDtypeStruct(placed.shape, placed.dtype),
        in_specs=[pl.BlockSpec(memory_space=pltpu.SMEM), pl.BlockSpec(memory_space=pltpu.VMEM)],
        out_specs=pl.BlockSpec(memory_space=pltpu.VMEM),
        name="unpack",
    )(spans, placed)


def assemble_kernel(failed_ref, spans_ref, own_ref, fresh0_ref, fresh1_ref, fresh2_ref, fresh3_ref, grads_ref, sent_ref, restored_ref):
    section = lax.axis_index("section")
    me = lax.axis_index("replica")
    here = failed_ref[section, lax.axis_index("tensor")] == me
    rows, width = own_ref.shape
    groups, _, cols = sent_ref.shape
    part = fresh0_ref.shape[0]
    apart = cols // SPAN
    spans = places(spans_ref, section, width // SPAN)
    for k, fresh_ref in enumerate((fresh0_ref, fresh1_ref, fresh2_ref, fresh3_ref)):
        at = pl.ds(pl.multiple_of(((me & 3) ^ k) * part, part), part)
        for n, (_, place) in enumerate(spans):
            block = jnp.where(here, fresh_ref[:, place], own_ref[at, n * SPAN : (n + 1) * SPAN])
            restored_ref[at, n * SPAN : (n + 1) * SPAN] = block
            sent_ref[n // apart, at, (n % apart) * SPAN : (n % apart + 1) * SPAN] = block
    for t in range(groups):
        total = grads_ref[0, t].astype(WIDE)
        for x in range(1, PLANE):
            total = total + grads_ref[x, t].astype(WIDE)
        sent_ref[t, rows:, :] = total.astype(SHORT)


def assemble(failed, spans, own, fresh, grads):
    rows, width = own.shape
    _, groups, part, cols = grads.shape
    return pl.pallas_call(
        assemble_kernel,
        out_shape=(
            jax.ShapeDtypeStruct((groups, rows + part, cols), SHORT),
            jax.ShapeDtypeStruct((rows, width), SHORT),
        ),
        in_specs=[pl.BlockSpec(memory_space=pltpu.SMEM)] * 2 + [pl.BlockSpec(memory_space=pltpu.VMEM)] * 6,
        out_specs=(pl.BlockSpec(memory_space=pltpu.VMEM),) * 2,
        name="assemble",
    )(failed, spans, own, *fresh, grads)


def adam(first, second, grad):
    one = 0.9 * first + 0.1 * grad
    two = 0.95 * second + 0.05 * (grad * grad)
    return one / (jnp.sqrt(two) + 1e-08)


def shards(activations, key_grads, weight, first_moment, second_moment, probe_matrix, failed_replica, resend_spans):
    copies = lax.axis_size("replica")
    my_replica = lax.axis_index("replica")
    my_section = lax.axis_index("section")
    my_tensor = lax.axis_index("tensor")
    failed = failed_replica[my_section, my_tensor]
    my_spans = resend_spans[my_section]
    own_weight = weight[0, 0]
    own_first = first_moment[0, 0]
    own_second = second_moment[0, 0]
    rows, width = own_weight.shape
    nchunk = width // 128
    is_failed = my_replica == failed
    part = rows // PLANE

    local = activations[0, 0]
    tokens, cols = local.shape
    squares = jnp.sum(jnp.square(local.astype(WIDE)), axis=1).reshape(-1, 128)
    squares = from_behind(squares, "section", 1).reshape(1, tokens)
    incoming = from_behind(local, "section", 1)
    x = incoming.astype(WIDE)

    mask = serve(failed_replica, resend_spans, own_weight, own_first, own_second)
    served = jnp.sum(exchange_x(mask).astype(WIDE), axis=0).astype(SHORT)

    high, low = two_halves(squares)
    extra = jnp.concatenate([high, low, jnp.zeros((6, tokens), SHORT)], axis=0)
    held = jnp.concatenate([tied(key_grads[0, 0].T, mask), extra], axis=0)
    held = doubled(doubled(held, my_tensor, 0), my_tensor, 1)
    held, served = lax.optimization_barrier((held, served))
    cross = width - my_spans.shape[0] * SPAN
    crossed = served[:, :, :cross] + swap(served[:, :, :cross], "replica", PLANE)
    fresh = jnp.concatenate([crossed, served[:, :, cross:]], axis=2)
    fresh_weight = [fresh[0]] + [swap(fresh[0], "replica", bit) for bit in (1, 2, 3)]
    held = doubled(held, my_tensor, 2).reshape(8, -1, tokens)
    kg_all = held[:, :rows].reshape(8 * rows, tokens)
    squares = jnp.sum(held[:, rows].astype(WIDE) + held[:, rows + 1].astype(WIDE), axis=0)
    inverse_rms = 1.0 / jnp.sqrt(squares / width + 1e-05)

    normed = (x * inverse_rms[:, None]).astype(SHORT)
    grad = lax.dot_general(kg_all, normed, (((1,), (0,)), ((), ())), preferred_element_type=WIDE).astype(SHORT)
    grad = grad.reshape(8, PLANE, part, cols).transpose(1, 0, 2, 3)
    grad = exchange_x(grad)

    sent, restored_weight = assemble(failed_replica, resend_spans, own_weight, fresh_weight, grad)
    own_first, own_second, restored_weight, fresh = lax.optimization_barrier((own_first, own_second, restored_weight, fresh))
    got = lax.all_to_all(sent, "tensor", 0, 0, tiled=True)
    weight_cols = got[:, :rows].reshape(8 * rows, cols)
    grad_rows = got[:, rows:].transpose(1, 0, 2).reshape(part, width)

    keys = lax.dot_general(weight_cols, normed, (((1,), (1,)), ((), ())), preferred_element_type=WIDE).astype(SHORT)
    weight_cols, keys, grad_rows = lax.optimization_barrier((weight_cols, keys, grad_rows))
    mean_rows = (grad_rows.astype(WIDE) + swap(grad_rows, "replica", PLANE).astype(WIDE)) / copies
    feature = lax.dot_general(kg_all, weight_cols, (((0,), (0,)), ((), ())), preferred_element_type=WIDE)
    product = jnp.sum(feature * x, axis=1).reshape(-1, 128)
    for bit in (1, 2, 4):
        product = product + swap(product, "tensor", bit)
    product = product.reshape(tokens, 1)
    scale = inverse_rms[:, None]
    input_grad = scale * feature - scale * scale * scale * x * product / width
    outgoing = from_behind(input_grad.astype(SHORT), "section", -1)
    got = lax.all_to_all(keys.reshape(8, rows, tokens), "tensor", 0, 0, tiled=True)
    key_out = jnp.sum(got.astype(WIDE), axis=0).T.astype(SHORT)

    def checksum(source):
        shaped = source.reshape(-1, nchunk, 128)
        mixed = jnp.einsum("jnc,cp->jnp", shaped, probe_matrix, precision=lax.Precision.HIGHEST)
        return mixed.reshape(-1, nchunk * probe_matrix.shape[1])

    fresh = unpack(resend_spans, fresh[1:]).astype(WIDE)
    fresh_update = adam(fresh[0], fresh[1], mean_rows).astype(SHORT)
    fresh_sums = checksum(fresh.reshape(2 * part, width)).astype(SHORT).reshape(2, width)
    shared = gather_x(jnp.concatenate([mean_rows.astype(SHORT), fresh_update, fresh_sums], axis=0))
    mean_grad = shared[:, :part].reshape(rows, width).astype(WIDE)
    fresh_update = shared[:, part : 2 * part].reshape(rows, width).astype(WIDE)
    fresh_sums = shared[:, 2 * part :].reshape(PLANE, 2, part, -1).transpose(1, 0, 2, 3).reshape(2, rows, -1).astype(WIDE)
    update = jnp.where(is_failed, fresh_update, adam(own_first, own_second, mean_grad))
    own_sums = jnp.stack([checksum(own_first), checksum(own_second)])
    checksums = jnp.where(is_failed, fresh_sums, own_sums)
    weight_checksums = checksum(restored_weight.astype(WIDE))
    return (key_out[None, None], outgoing[None, None], update[None, None], checksums[None, None], weight_checksums[None, None])


def solution(mesh):
    by_rows = P("replica", "section", "tensor", None)
    by_features = P("replica", "section", None, "tensor")
    return jax.shard_map(
        shards,
        mesh=mesh,
        in_specs=(by_features, by_features, by_rows, by_rows, by_rows, P(), P(), P()),
        out_specs=(by_features, by_features, by_rows, P("replica", "section", None, "tensor", None), by_rows),
        check_vma=False,
    )
```
